128 devices in a mesh: seq: 16 (over x_lo, z, core), head: 8 (over x_hi, y).
Axes of the slice: x: 4 (x_hi: 2, x_lo: 2; x = x_hi * 2 + x_lo), y: 4, z: 4, core: 2. Of those that a mesh axis runs over, the one named last changes fastest.
Arguments:
- tokens: bfloat16 [8192, 5120], P('seq'), may hold values from -6 to 6
- shift_vector: float32 [5120], replicated, may hold values from -3 to 3
- scale_vector: float32 [5120], replicated, may hold values from -3 to 3
- query_weight: bfloat16 [5120, 3072], P(None, 'head'), may hold values from -0.078125 to 0.078125
- key_weight: bfloat16 [5120, 3072], P(None, 'head'), may hold values from -0.078125 to 0.078125
- value_weight: bfloat16 [5120, 3072], P(None, 'head'), may hold values from -0.078125 to 0.078125
- query_gain: float32 [3072], P('head'), may hold values from 0.8 to 1.8
- key_gain: float32 [3072], P('head'), may hold values from 0.8 to 1.8
- out_weight: bfloat16 [3072, 5120], P('head'), may hold values from -1.75 to 1.75
Outputs:
- attn_out: bfloat16 [8192, 5120], P('seq', 'head')
The draws below stay inside these ranges and needn't reach their ends.
All inputs are finite; a program needn't handle non-finite values.
Results may differ from the reference program's by a relative error of at most 0.02.
Values may be sent and summed in bfloat16 or wider, within the bound.
No kernel may reach another device: no remote copies, remote signals or barrier semaphores. Data moves between devices by JAX's collectives and lax.ppermute only.
A program may use at most 128 MiB of HBM per device.

```python
import math
import jax
import jax.numpy as jnp
from jax import lax

D = 5120
HD = 128
HEADS = 24
TOKENS = 8192
N_HEAD = 8


def block_scale(rng, shape, shards, least, largest):
    gain, own = 1.0, jax.random.fold_in(rng, 6)
    for axis_at, blocks in shards:
        draws = jnp.exp(jax.random.uniform(jax.random.fold_in(own, axis_at), (blocks,), jnp.float32, least / len(shards), largest / len(shards)))
        gain = gain * jnp.repeat(draws, shape[axis_at] // blocks).reshape([-1 if axis == axis_at else 1 for axis in range(len(shape))])
    return gain


def noise(key, shape, scale, bound, pieces=(), held_as=jnp.bfloat16):
    array = jax.random.normal(key, shape, jnp.float32) * scale
    if len(pieces) > 0:
        array = block_scale(key, shape, pieces, -0.22, 0.18) * array
    return jnp.clip(array, min=-bound, max=bound).astype(held_as)


def setup_inputs(seed: int = 0) -> dict:
    key_of = jax.random.split(jax.random.key(seed), 10)
    return {
        "tokens": noise(key_of[0], (TOKENS, D), 1.0, 6.0, ((0, 16),)),
        "shift_vector": noise(key_of[1], (D,), 0.5, 3.0, (), jnp.float32),
        "scale_vector": noise(key_of[2], (D,), 0.5, 3.0, (), jnp.float32),
        "query_weight": noise(key_of[3], (D, HEADS * HD), D ** -0.5, 0.078125, ((1, 8),)),
        "key_weight": noise(key_of[4], (D, HEADS * HD), D ** -0.5, 0.078125, ((1, 8),)),
        "value_weight": noise(key_of[5], (D, HEADS * HD), D ** -0.5, 0.078125, ((1, 8),)),
        "query_gain": jnp.clip(0.8 + 0.99999994 * jax.random.uniform(key_of[6], (HEADS * HD,), jnp.float32) ** block_scale(key_of[6], (HEADS * HD,), ((0, 8),), -0.2, 0.2), 0.8, 1.8),
        "key_gain": jnp.clip(0.8 + 0.99999994 * jax.random.uniform(key_of[7], (HEADS * HD,), jnp.float32) ** block_scale(key_of[7], (HEADS * HD,), ((0, 8),), -0.2, 0.2), 0.8, 1.8),
        "out_weight": noise(key_of[8], (HEADS * HD, D), (max(HEADS * HD // 256, 1)) ** -0.5, 1.75, ((0, 8),)),
    }


softcap = 10.0
epsilon = 1e-06

def modulate(tokens, shift_vector, scale_vector):
    values = tokens.astype(jnp.float32)
    center = lax.optimization_barrier(jnp.mean(values, axis=-1, keepdims=True))
    spread = lax.optimization_barrier(jnp.mean(jnp.square(values - center), axis=-1, keepdims=True))
    normed = (values - center) * lax.rsqrt(spread + epsilon)
    return (normed * (1.0 + scale_vector) + shift_vector).astype(jnp.bfloat16)

def head_norm(projected, gain_vector):
    shaped = projected.reshape(projected.shape[0], -1, HD)
    mean_sq = lax.optimization_barrier(jnp.mean(jnp.square(shaped), axis=-1, keepdims=True))
    gain_rows = gain_vector.reshape(-1, HD)
    return (shaped * lax.rsqrt(mean_sq + epsilon) * gain_rows).astype(jnp.bfloat16)

def capped_weights(scores):
    return jnp.exp(softcap * jnp.tanh(scores / (math.sqrt(HD) * softcap)) - softcap)

def reference(tokens, shift_vector, scale_vector, query_weight, key_weight, value_weight, query_gain, key_gain, out_weight):
    normed = modulate(tokens, shift_vector, scale_vector)
    queries = head_norm(jnp.dot(normed, query_weight, preferred_element_type=jnp.float32), query_gain)
    keys_all = head_norm(jnp.dot(normed, key_weight, preferred_element_type=jnp.float32), key_gain)
    values_all = jnp.dot(normed, value_weight, preferred_element_type=jnp.float32).astype(jnp.bfloat16)
    values_all = values_all.reshape(TOKENS, HEADS, HD)

    def one_head(triple):
        head_query, head_key, head_value = triple
        scores = jnp.dot(head_query, head_key.T, preferred_element_type=jnp.float32)
        weights = capped_weights(scores)
        totals = lax.optimization_barrier(jnp.sum(weights, axis=1, keepdims=True))
        mixture = jnp.dot(weights.astype(jnp.bfloat16), head_value, preferred_element_type=jnp.float32)
        return (mixture / totals).astype(jnp.bfloat16)
    attended = lax.map(one_head, (jnp.swapaxes(queries, 0, 1), jnp.swapaxes(keys_all, 0, 1), jnp.swapaxes(values_all, 0, 1)))
    attended = jnp.swapaxes(attended, 0, 1).reshape(TOKENS, HEADS * HD)
    group_width = HEADS * HD // N_HEAD
    result = jnp.zeros((TOKENS, D), jnp.float32)
    for member in range(N_HEAD):
        lower = member * group_width
        partial_out = jnp.dot(attended[:, lower:lower + group_width], out_weight[lower:lower + group_width], preferred_element_type=jnp.float32).astype(jnp.bfloat16)
        partial_out = lax.optimization_barrier(partial_out)
        result = result + partial_out.astype(jnp.float32)
    return result.astype(jnp.bfloat16)
```

```python
import functools
import math

import jax
import jax.numpy as jnp
from jax import lax
from jax.experimental import pallas as pl
from jax.experimental.pallas import tpu as pltpu
from jax.sharding import PartitionSpec as P

HD = 128
SOFTCAP = 10.0
EPSILON = 1e-06
GROUP_HEADS = 3
WIDE = GROUP_HEADS * HD
ROWS = 512
D = 5120
OUT_COLS = 640
BK = 512
EXP_SCALE = SOFTCAP * math.log2(math.e)
SCORE_SCALE = 1.0 / (SOFTCAP * math.sqrt(HD))
VMEM = 56 * 2**20

BF16 = jnp.bfloat16
F32 = jnp.float32


def seq_perm(move):
    pairs = []
    for i in range(16):
        x, z, c = move(i // 8, (i // 2) % 4, i % 2)
        pairs.append((i, x * 8 + (z % 4) * 2 + c))
    return pairs


def head_perm(move):
    pairs = []
    for i in range(8):
        x, y = move(i // 4, i % 4)
        pairs.append((i, x * 4 + (y % 4)))
    return pairs


SWAP_CORE = seq_perm(lambda x, z, c: (x, z, 1 - c))
SWAP_X = seq_perm(lambda x, z, c: (1 - x, z, c))
Z_UP = seq_perm(lambda x, z, c: (x, z + 1, c))
Z_DOWN = seq_perm(lambda x, z, c: (x, z - 1, c))
SWAP_XHI = head_perm(lambda x, y: (1 - x, y))
Y_STEP = [None] + [head_perm(lambda x, y, r=r: (x, y + r)) for r in (1, 2, 3)]


def params(flops=0):
    return pltpu.CompilerParams(vmem_limit_bytes=VMEM)


def cost(flops, nbytes, trans=0):
    return pl.CostEstimate(flops=int(flops), bytes_accessed=int(nbytes), transcendentals=int(trans))


def qkv_kernel(tok, shift, scale, wq, wk, wv, gq, gk, q_o, kv0, kv1, kv2, mean_s, rstd_s, n_s, aq, ak, av):
    j = pl.program_id(0)
    nk = pl.num_programs(0)

    def normalise(block, slot):
        cols = pl.ds(pl.multiple_of(block * BK, BK), BK)
        xb = tok[:, cols].astype(F32)
        m = jnp.concatenate([mean_s[...]] * (BK // 128), axis=1)
        r = jnp.concatenate([rstd_s[...]] * (BK // 128), axis=1)
        y = (xb - m) * r
        n_s[slot] = (y * (1.0 + scale[:, cols]) + shift[:, cols]).astype(BF16)

    @pl.when(j == 0)
    def _():
        def stats(i, carry):
            rows = pl.ds(pl.multiple_of(i * 32, 32), 32)
            x = tok[rows, :].astype(F32)
            mean = jnp.sum(x, axis=1, keepdims=True) * (1.0 / D)
            cen = x - mean
            var = jnp.sum(cen * cen, axis=1, keepdims=True) * (1.0 / D)
            mean_s[rows, :] = jnp.broadcast_to(mean, (32, 128))
            rstd_s[rows, :] = jnp.broadcast_to(lax.rsqrt(var + EPSILON), (32, 128))
            return carry

        lax.fori_loop(0, ROWS // 32, stats, 0, unroll=4)
        normalise(0, 0)
        aq[...] = jnp.zeros_like(aq)
        ak[...] = jnp.zeros_like(ak)
        av[...] = jnp.zeros_like(av)

    n = n_s[j % 2]
    aq[...] += jnp.dot(n, wq[...], preferred_element_type=F32)
    ak[...] += jnp.dot(n, wk[...], preferred_element_type=F32)
    av[...] += jnp.dot(n, wv[...], preferred_element_type=F32)
    normalise(jnp.minimum(j + 1, nk - 1), (j + 1) % 2)

    @pl.when(j == nk - 1)
    def _():
        for h, kv in enumerate((kv0, kv1, kv2)):
            cols = slice(h * HD, (h + 1) * HD)

            def unit(a):
                return a * lax.rsqrt(jnp.mean(a * a, axis=1, keepdims=True) + EPSILON)

            q_o[:, cols] = (unit(aq[:, cols]) * (gq[:, cols] * SCORE_SCALE)).astype(BF16)
            kv[:, :HD] = (unit(ak[:, cols]) * gk[:, cols]).astype(BF16)
            kv[:, HD:] = av[:, cols].astype(BF16)


def project(tokens, shift, scale, wq, wk, wv, gq, gk):
    nk = D // BK
    whole = lambda shape: pl.BlockSpec(shape, lambda j: (0, 0))
    wspec = pl.BlockSpec((BK, WIDE), lambda j: (j, 0))
    return pl.pallas_call(
        qkv_kernel,
        grid=(nk,),
        in_specs=[whole((ROWS, D)), whole((1, D)), whole((1, D)), wspec, wspec, wspec,
                  whole((1, WIDE)), whole((1, WIDE))],
        out_specs=[whole((ROWS, WIDE))] + [whole((ROWS, 2 * HD))] * 3,
        out_shape=[jax.ShapeDtypeStruct((ROWS, WIDE), BF16)]
        + [jax.ShapeDtypeStruct((ROWS, 2 * HD), BF16)] * 3,
        scratch_shapes=[
            pltpu.VMEM((ROWS, 128), F32),
            pltpu.VMEM((ROWS, 128), F32),
            pltpu.VMEM((2, ROWS, BK), BF16),
            pltpu.VMEM((ROWS, WIDE), F32),
            pltpu.VMEM((ROWS, WIDE), F32),
            pltpu.VMEM((ROWS, WIDE), F32),
        ],
        compiler_params=params(),
        cost_estimate=cost(2 * ROWS * D * WIDE * 3, 18e6),
        name="qkv",
    )(tokens, shift.reshape(1, D), scale.reshape(1, D), wq, wk, wv, gq.reshape(1, WIDE), gk.reshape(1, WIDE))


def attend_kernel(q0, q1, q2, q3, k0, k1, k2, k3, k4, keep, send):
    chunks = []
    for kv in (k0, k1, k2, k3, k4):
        for s in range(0, kv.shape[0], 256):
            chunks.append((kv, s))
    for q, out, base in ((q0, keep, 0), (q1, send, 0), (q2, keep, ROWS), (q3, send, ROWS)):
        qq = q[...]
        acc = None
        for kv, s in chunks:
            k = kv[s : s + 256, :HD]
            v = kv[s : s + 256, HD:]
            x = lax.dot_general(qq, k, (((1,), (1,)), ((), ())), preferred_element_type=F32)
            p = jnp.exp2(EXP_SCALE * jnp.tanh(x)).astype(BF16)
            d = jnp.dot(p, jnp.concatenate([v, jnp.ones_like(v)], axis=1), preferred_element_type=F32)
            acc = d if acc is None else acc + d
        out[base : base + ROWS, :] = acc.astype(BF16)


def attend(qs, kvs, h):
    whole = lambda shape: pl.BlockSpec(shape, lambda i: (0, 0))
    return pl.pallas_call(
        attend_kernel,
        grid=(1,),
        in_specs=[pl.BlockSpec((ROWS, HD), lambda i: (0, h))] * 4 + [whole(kv.shape) for kv in kvs],
        out_specs=[whole((2 * ROWS, 2 * HD))] * 2,
        out_shape=[jax.ShapeDtypeStruct((2 * ROWS, 2 * HD), BF16)] * 2,
        compiler_params=params(),
        cost_estimate=cost(4 * 2048 * 2048 * 256, 3e6, 2 * 2048 * 2048),
        name="attend",
    )(*qs, *kvs)


def combine_core_kernel(keep, recv, mine, away):
    a = keep[:ROWS, :].astype(F32) + recv[:ROWS, :].astype(F32)
    mine[...] = a
    b = keep[ROWS:, :].astype(F32) + recv[ROWS:, :].astype(F32)
    away[:ROWS, :] = b[:, :HD].astype(BF16)
    for p in range(ROWS // 128):
        t = jnp.transpose(b[p * 128 : (p + 1) * 128, HD:])
        away[ROWS + 16 * p : ROWS + 16 * (p + 1), :] = t[:16].astype(BF16)


def combine_core(keep, recv):
    return pl.pallas_call(
        combine_core_kernel,
        out_shape=[jax.ShapeDtypeStruct((ROWS, 2 * HD), F32), jax.ShapeDtypeStruct((ROWS + 64, HD), BF16)],
        compiler_params=params(),
        cost_estimate=cost(1e6, 2e6),
        name="combine_core",
    )(keep, recv)


def combine_x_kernel(mine, recv, out):
    for p in range(ROWS // 128):
        rows = slice(p * 128, (p + 1) * 128)
        t = recv[ROWS + 16 * p : ROWS + 16 * (p + 1), :].astype(F32)[:1]
        total = mine[rows, HD:] + jnp.transpose(jnp.broadcast_to(t, (128, 128)))
        out[rows, :] = ((mine[rows, :HD] + recv[rows, :].astype(F32)) / total).astype(BF16)


def combine_x(mine, recv):
    return pl.pallas_call(
        combine_x_kernel,
        out_shape=jax.ShapeDtypeStruct((ROWS, HD), BF16),
        compiler_params=params(),
        cost_estimate=cost(1e6, 1e6),
        name="combine_x",
    )(mine, recv)


def out_kernel(core, *refs):
    a = refs[:12]
    first = refs[12:16]
    second = refs[16:20]
    keep, send = refs[20:]
    acc = None
    for r in range(4):
        w = jnp.concatenate([first[r][...], second[r][...]], axis=1)
        for h in range(3):
            d = jnp.dot(a[3 * r + h][...], w[h * HD : (h + 1) * HD], preferred_element_type=F32)
            acc = d if acc is None else acc + d
    lead = core[0] == 0
    keep[...] = jnp.where(lead, acc[:, :128], acc[:, 128:])
    send[...] = jnp.where(lead, acc[:, 128:], acc[:, :128]).astype(BF16)


def out_project(core, attended, first, second):
    whole = pl.BlockSpec((ROWS, HD), lambda j: (0, 0))
    wspec = pl.BlockSpec((WIDE, 128), lambda j: (0, j))
    ospec = pl.BlockSpec((ROWS, 128), lambda j: (0, j))
    return pl.pallas_call(
        out_kernel,
        grid=(OUT_COLS // 128,),
        in_specs=[pl.BlockSpec(memory_space=pltpu.SMEM)] + [whole] * 12 + [wspec] * 8,
        out_specs=[ospec, ospec],
        out_shape=[jax.ShapeDtypeStruct((ROWS, OUT_COLS), F32), jax.ShapeDtypeStruct((ROWS, OUT_COLS), BF16)],
        compiler_params=params(),
        cost_estimate=cost(2 * ROWS * 1536 * 1280, 8e6),
        name="out_project",
    )(core.reshape(1), *attended, *first, *second)


def shards(tokens, shift, scale, wq, wk, wv, gq, gk, wo):
    seq = lax.axis_index("seq")
    head = lax.axis_index("head")
    core = seq % 2
    x_hi, y = head // 4, head % 4

    def columns(side, r):
        col = ((x_hi + side) % 2) * 4 + (y + r) % 4
        return lax.dynamic_slice(wo, (0, col * OUT_COLS), (WIDE, OUT_COLS))

    first = [columns(core, 0)]
    for r in (1, 2, 3):
        first.append(lax.ppermute(columns(core, r), "head", Y_STEP[r]))
    second = [columns(1 - core, 0)]
    for r in (1, 2, 3):
        second.append(lax.ppermute(first[r], "seq", SWAP_CORE))

    q, *kvs = project(tokens, shift, scale, wq, wk, wv, gq, gk)
    q_core = lax.ppermute(q, "seq", SWAP_CORE)
    q_x = lax.ppermute(q, "seq", SWAP_X)
    q_xc = lax.ppermute(q_x, "seq", SWAP_CORE)
    qs = (q, q_core, q_x, q_xc)

    gathered = [[], [], [], []]
    for h in range(GROUP_HEADS):
        kv = kvs[h]
        below = lax.ppermute(kv, "seq", Z_UP)
        above = lax.ppermute(kv, "seq", Z_DOWN)
        far_a = lax.ppermute(below[:256], "seq", Z_UP)
        far_b = lax.ppermute(above[256:], "seq", Z_DOWN)
        keep, send = attend(qs, (kv, below, above, far_a, far_b), h)
        mine, away = combine_core(keep, lax.ppermute(send, "seq", SWAP_CORE))
        att = combine_x(mine, lax.ppermute(away, "seq", SWAP_X))
        gathered[0].append(att)
        for r in (1, 2, 3):
            gathered[r].append(lax.ppermute(att, "head", Y_STEP[r]))
    keep, send = out_project(core, [a for rel in gathered for a in rel], first, second)
    other = lax.ppermute(send, "head", SWAP_XHI)
    return (keep + other.astype(F32)).astype(BF16)


def solution(mesh):
    in_specs = (
        P("seq", None),
        P(),
        P(),
        P(None, "head"),
        P(None, "head"),
        P(None, "head"),
        P("head"),
        P("head"),
        P("head", None),
    )
    out_specs = P("seq", "head")
    return jax.shard_map(shards, mesh=mesh, in_specs=in_specs, out_specs=out_specs, check_vma=False)
```

```python
import functools
import math

import jax
import jax.numpy as jnp
from jax import lax
from jax.experimental import pallas as pl
from jax.experimental.pallas import tpu as pltpu
from jax.sharding import PartitionSpec as P

HD = 128
SOFTCAP = 10.0
EPSILON = 1e-06
GROUP_HEADS = 3
WIDE = GROUP_HEADS * HD
ROWS = 512
D = 5120
OUT_COLS = 640
TOK_PARTS = 4
HALF = ROWS // 2
PACK = HALF + HALF // 8
EXP_SCALE = SOFTCAP * math.log2(math.e)
SCORE_SCALE = 1.0 / (SOFTCAP * math.sqrt(HD))

BF16 = jnp.bfloat16
F32 = jnp.float32


def seq_perm(move):
    pairs = []
    for i in range(16):
        x, z, c = move(i // 8, (i // 2) % 4, i % 2)
        pairs.append((i, x * 8 + (z % 4) * 2 + c))
    return pairs


def head_perm(move):
    pairs = []
    for i in range(8):
        x, y = move(i // 4, i % 4)
        pairs.append((i, x * 4 + (y % 4)))
    return pairs


SWAP_CORE = seq_perm(lambda x, z, c: (x, z, 1 - c))
SWAP_X = seq_perm(lambda x, z, c: (1 - x, z, c))
Z_UP = seq_perm(lambda x, z, c: (x, z + 1, c))
Z_DOWN = seq_perm(lambda x, z, c: (x, z - 1, c))
SWAP_XHI = head_perm(lambda x, y: (1 - x, y))
Y_STEP = [None] + [head_perm(lambda x, y, r=r: (x, y + r)) for r in (1, 2, 3)]


def params(mib=8):
    return pltpu.CompilerParams(vmem_limit_bytes=mib * 2**20)


def cost(flops, nbytes, trans=0):
    return pl.CostEstimate(flops=int(flops), bytes_accessed=int(nbytes), transcendentals=int(trans))


def unit(a):
    return a * lax.rsqrt(jnp.mean(a * a, axis=1, keepdims=True) + EPSILON)


def kv_kernel(tok, shift_h, scale_h, wk, wv, gk_h, kv_o, n_o, tok_v, n_s, wk_v, wv_v, shift, scale, gk, tsem, wsem, nsem, vsem):
    tiles = D // 128
    part = ROWS // TOK_PARTS

    def rows_of(i):
        return pl.ds(i * part, part)

    tok_in = [pltpu.make_async_copy(tok.at[rows_of(i)], tok_v.at[rows_of(i)], tsem.at[i]) for i in range(TOK_PARTS)]
    n_out = [pltpu.make_async_copy(n_s.at[rows_of(i)], n_o.at[rows_of(i)], nsem.at[i]) for i in range(TOK_PARTS)]
    w_in = [pltpu.make_async_copy(w, dst, wsem.at[i]) for i, (w, dst) in enumerate(((wk, wk_v), (wv, wv_v)))]
    vec_in = [
        pltpu.make_async_copy(src, dst, vsem.at[i])
        for i, (src, dst) in enumerate(((shift_h, shift), (scale_h, scale), (gk_h, gk)))
    ]
    for c in vec_in + tok_in:
        c.start()
    for c in vec_in:
        c.wait()

    for p in range(TOK_PARTS):
        tok_in[p].wait()
        if p == TOK_PARTS - 2:
            for c in w_in:
                c.start()

        def stats(i, carry, p=p):
            rows = pl.ds(pl.multiple_of(p * part + i * 32, 32), 32)
            base = tok_v[rows, :128].astype(F32)
            s1 = jnp.zeros((32, 128), F32)
            s2 = jnp.zeros((32, 128), F32)
            for t in range(1, tiles):
                d = tok_v[rows, t * 128 : (t + 1) * 128].astype(F32) - base
                s1 = s1 + d
                s2 = s2 + d * d
            low = s1 * (1.0 / tiles)
            lane_mean = base + low
            mean = jnp.sum(lane_mean, axis=1, keepdims=True) * (1.0 / 128)
            off = lane_mean - mean
            var = jnp.sum(s2 - s1 * low + tiles * (off * off), axis=1, keepdims=True) * (1.0 / D)
            m = jnp.broadcast_to(mean, (32, 128))
            r = jnp.broadcast_to(lax.rsqrt(var + EPSILON), (32, 128))
            for t in range(tiles):
                cols = slice(t * 128, (t + 1) * 128)
                y = (tok_v[rows, cols].astype(F32) - m) * r
                n_s[rows, cols] = (y * (1.0 + scale[:, cols]) + shift[:, cols]).astype(BF16)
            return carry

        lax.fori_loop(0, part // 32, stats, 0, unroll=2)
        n_out[p].start()
    for c in w_in:
        c.wait()
    for h in range(GROUP_HEADS):
        cols = slice(h * HD, (h + 1) * HD)
        w = jnp.concatenate([wk_v[:, cols], wv_v[:, cols]], axis=1)
        d = jnp.dot(n_s[...], w, preferred_element_type=F32)
        at = 2 * h * HD
        kv_o[:, at : at + HD] = (unit(d[:, :HD]) * gk[cols].reshape(1, HD)).astype(BF16)
        kv_o[:, at + HD : at + 2 * HD] = d[:, HD:].astype(BF16)
    for c in n_out:
        c.wait()


def project_kv(tokens, shift, scale, wk, wv, gk):
    hbm = pl.BlockSpec(memory_space=pltpu.HBM)
    vmem = pl.BlockSpec(memory_space=pltpu.VMEM)
    return pl.pallas_call(
        kv_kernel,
        in_specs=[hbm] * 6,
        out_specs=[vmem, hbm],
        out_shape=[jax.ShapeDtypeStruct((ROWS, 2 * WIDE), BF16), jax.ShapeDtypeStruct((ROWS, D), BF16)],
        scratch_shapes=[
            pltpu.VMEM((ROWS, D), BF16),
            pltpu.VMEM((ROWS, D), BF16),
            pltpu.VMEM((D, WIDE), BF16),
            pltpu.VMEM((D, WIDE), BF16),
            pltpu.VMEM((1, D), F32),
            pltpu.VMEM((1, D), F32),
            pltpu.VMEM((WIDE,), F32),
            pltpu.SemaphoreType.DMA((TOK_PARTS,)),
            pltpu.SemaphoreType.DMA((2,)),
            pltpu.SemaphoreType.DMA((TOK_PARTS,)),
            pltpu.SemaphoreType.DMA((3,)),
        ],
        compiler_params=params(56),
        cost_estimate=cost(2 * ROWS * D * WIDE * 2, 18e6),
        name="project_kv",
    )(tokens, shift.reshape(1, D), scale.reshape(1, D), wk, wv, gk)


def q_kernel(cols, n_h, wq_h, gq_h, wo, q_o, o0, o1, o2, o3, o4, n, wq, gq, blocks, isem, bsem, osem):
    halves = [pl.ds(i * HALF, HALF) for i in range(2)]
    gain_in = pltpu.make_async_copy(gq_h, gq, isem.at[0])
    w_in = pltpu.make_async_copy(wq_h, wq, isem.at[1])
    n_in = [pltpu.make_async_copy(n_h.at[rows], n.at[rows], isem.at[2 + i]) for i, rows in enumerate(halves)]
    outs = (o0, o1, o2, o3, o4)
    block_in = [
        pltpu.make_async_copy(wo.at[:, pl.ds(pl.multiple_of(cols[i] * 128, 128), OUT_COLS)], blocks.at[i], bsem.at[i])
        for i in range(5)
    ]
    block_out = [pltpu.make_async_copy(blocks.at[i], outs[i], osem.at[i]) for i in range(5)]
    for c in [gain_in, w_in] + n_in + block_in:
        c.start()
    gain_in.wait()
    w_in.wait()
    for i in range(2):
        n_in[i].wait()
        rows = slice(i * HALF, (i + 1) * HALF)
        d = jnp.dot(n[rows, :], wq[...], preferred_element_type=F32)
        for h in range(GROUP_HEADS):
            at = slice(h * HD, (h + 1) * HD)
            q_o[rows, at] = (unit(d[:, at]) * (gq[at] * SCORE_SCALE).reshape(1, HD)).astype(BF16)
        for j in range(5):
            if i == 0:
                block_in[j].wait()
                block_out[j].start()
    for c in block_out:
        c.wait()


def project_q(cols, n, wq, gq, wo):
    hbm = pl.BlockSpec(memory_space=pltpu.HBM)
    return pl.pallas_call(
        q_kernel,
        in_specs=[pl.BlockSpec(memory_space=pltpu.SMEM)] + [hbm] * 4,
        out_specs=[pl.BlockSpec(memory_space=pltpu.VMEM)] + [hbm] * 5,
        out_shape=[jax.ShapeDtypeStruct((ROWS, WIDE), BF16)] + [jax.ShapeDtypeStruct((WIDE, OUT_COLS), BF16)] * 5,
        scratch_shapes=[
            pltpu.VMEM((ROWS, D), BF16),
            pltpu.VMEM((D, WIDE), BF16),
            pltpu.VMEM((WIDE,), F32),
            pltpu.VMEM((5, WIDE, OUT_COLS), BF16),
            pltpu.SemaphoreType.DMA((4,)),
            pltpu.SemaphoreType.DMA((5,)),
            pltpu.SemaphoreType.DMA((5,)),
        ],
        compiler_params=params(60),
        cost_estimate=cost(2 * ROWS * D * WIDE, 14e6),
        name="project_q",
    )(cols, n, wq, gq, wo)


def mix(qq, kvs, chunk):
    acc = None
    for kv in kvs:
        for s in range(0, kv.shape[0], chunk):
            k = kv[s : s + chunk, :HD]
            v = kv[s : s + chunk, HD:]
            x = lax.dot_general(qq, k, (((1,), (1,)), ((), ())), preferred_element_type=F32)
            p = jnp.exp2(EXP_SCALE * jnp.tanh(x)).astype(BF16)
            d = jnp.dot(p, jnp.concatenate([v, jnp.ones_like(v)], axis=1), preferred_element_type=F32)
            acc = d if acc is None else acc + d
    return acc


def first_kernel(q0, q1, q2, k0, k1, k2, part0, part1):
    for i, q in enumerate((q0, q1, q2)):
        acc = mix(q[...], (k0, k1, k2), 256)
        for half, part in enumerate((part0, part1)):
            rows = acc[half * HALF : (half + 1) * HALF]
            at = i * PACK
            part[at : at + HALF, :] = rows[:, :HD].astype(BF16)
            for p in range(HALF // 128):
                t = jnp.transpose(rows[p * 128 : (p + 1) * 128, HD:])
                to = at + HALF + 16 * p
                part[to : to + 16, :] = t[:16].astype(BF16)


def attend_first(qs, kvs):
    head = lambda rows, cols: pl.BlockSpec((rows, cols), lambda h: (0, h))
    return pl.pallas_call(
        first_kernel,
        grid=(GROUP_HEADS,),
        in_specs=[head(ROWS, HD)] * 3 + [head(ROWS, 2 * HD)] * 3,
        out_specs=[head(3 * PACK, HD)] * 2,
        out_shape=[jax.ShapeDtypeStruct((3 * PACK, WIDE), BF16)] * 2,
        compiler_params=params(24),
        cost_estimate=cost(3 * 4 * 1536 * 1536 * 256, 6e6, 3 * 2 * 1536 * 1536),
        name="attend_first",
    )(*qs, *kvs)


def last_kernel(q0, q1, q2, q3, n0, n1, n2, k0, k1, part, keep, send):
    for h in range(GROUP_HEADS):
        col = slice(h * HD, (h + 1) * HD)
        wide = slice(2 * h * HD, 2 * (h + 1) * HD)
        for i, (q, out, base) in enumerate(((q0, keep, 0), (q1, send, 0), (q2, keep, PACK), (q3, send, PACK))):
            far = (k0[:, wide], k1[:, wide])
            if i == 3:
                acc = mix(q[:, col], (n0[:, wide], n1[:, wide], n2[:, wide]) + far, 256)
                mixture, totals = acc[:, :HD], None
            else:
                acc = mix(q[:, col], far, 256)
                old = part[i * PACK : (i + 1) * PACK, col].astype(F32)
                mixture, totals = acc[:, :HD] + old[:HALF], old[HALF:]
            out[base : base + HALF, col] = mixture.astype(BF16)
            for p in range(HALF // 128):
                t = jnp.transpose(acc[p * 128 : (p + 1) * 128, HD:])[:16]
                if totals is not None:
                    t = t + totals[16 * p : 16 * (p + 1)]
                at = base + HALF + 16 * p
                out[at : at + 16, col] = t.astype(BF16)


def attend_last(half, qs, kvs, part):
    whole = lambda shape: pl.BlockSpec(shape, lambda j: (0, 0))
    return pl.pallas_call(
        last_kernel,
        grid=(1,),
        in_specs=[pl.BlockSpec((HALF, WIDE), lambda j: (half, 0))] * 4
        + [whole((ROWS, 2 * WIDE))] * 3
        + [whole((256, 2 * WIDE))] * 2
        + [whole((3 * PACK, WIDE))],
        out_specs=[whole((2 * PACK, WIDE))] * 2,
        out_shape=[jax.ShapeDtypeStruct((2 * PACK, WIDE), BF16)] * 2,
        compiler_params=params(24),
        cost_estimate=cost(3 * 4 * 1024 * 1024 * 256, 4e6, 3 * 2 * 1024 * 1024),
        name="attend_last",
    )(*qs, *kvs, part)


def combine_core_kernel(keep, recv, mine, away):
    total = keep[...].astype(F32) + recv[...].astype(F32)
    mine[...] = total[:PACK].astype(BF16)
    away[...] = total[PACK:].astype(BF16)


def combine_core(keep, recv):
    return pl.pallas_call(
        combine_core_kernel,
        out_shape=[jax.ShapeDtypeStruct((PACK, WIDE), BF16)] * 2,
        compiler_params=params(),
        cost_estimate=cost(1e6, 2e6),
        name="combine_core",
    )(keep, recv)


def combine_x_kernel(mine, recv, out):
    total = mine[...].astype(F32) + recv[...].astype(F32)
    for h in range(GROUP_HEADS):
        cols = slice(h * HD, (h + 1) * HD)
        for p in range(HALF // 128):
            rows = slice(p * 128, (p + 1) * 128)
            t = total[HALF + 16 * p : HALF + 16 * p + 1, cols]
            out[rows, cols] = (total[rows, cols] / jnp.transpose(jnp.broadcast_to(t, (128, 128)))).astype(BF16)


def combine_x(mine, recv):
    return pl.pallas_call(
        combine_x_kernel,
        out_shape=jax.ShapeDtypeStruct((HALF, WIDE), BF16),
        compiler_params=params(),
        cost_estimate=cost(1e6, 1e6),
        name="combine_x",
    )(mine, recv)


def out_kernel(core, *refs):
    a = refs[:4]
    first = refs[4:8]
    second = refs[8:12]
    keep, send = refs[12:]
    rows = jnp.concatenate([piece[...] for piece in a], axis=1)
    lead = core[0] == 0
    for t in range(OUT_COLS // 128):
        col = slice(t * 128, (t + 1) * 128)
        w = jnp.concatenate(
            [jnp.concatenate([first[r][:, col], second[r][:, col]], axis=1) for r in range(4)], axis=0
        )
        acc = jnp.dot(rows, w, preferred_element_type=F32)
        keep[:, col] = jnp.where(lead, acc[:, :128], acc[:, 128:]).astype(BF16)
        send[:, col] = jnp.where(lead, acc[:, 128:], acc[:, :128]).astype(BF16)


def out_project(core, attended, first, second):
    vmem = pl.BlockSpec(memory_space=pltpu.VMEM)
    return pl.pallas_call(
        out_kernel,
        in_specs=[pl.BlockSpec(memory_space=pltpu.SMEM)] + [vmem] * 12,
        out_specs=[vmem, vmem],
        out_shape=[jax.ShapeDtypeStruct((HALF, OUT_COLS), BF16)] * 2,
        compiler_params=params(16),
        cost_estimate=cost(2 * HALF * 1536 * 1280, 6e6),
        name="out_project",
    )(core.reshape(1), *attended, *first, *second)


def final_kernel(keep, recv, *rest):
    rest[-1][...] = (keep[...].astype(F32) + recv[...].astype(F32)).astype(BF16)


def finish(half, keep, recv, out=None):
    whole = pl.BlockSpec((HALF, OUT_COLS), lambda j: (0, 0))
    return pl.pallas_call(
        final_kernel,
        grid=(1,),
        in_specs=[whole] * 2 + ([] if out is None else [pl.BlockSpec(memory_space=pl.ANY)]),
        out_specs=pl.BlockSpec((HALF, OUT_COLS), lambda j: (half, 0)),
        out_shape=jax.ShapeDtypeStruct((ROWS, OUT_COLS), BF16),
        input_output_aliases={} if out is None else {2: 0},
        compiler_params=params(8),
        cost_estimate=cost(1e6, 1e6),
        name="finish",
    )(*([keep, recv] if out is None else [keep, recv, out]))


def shards(tokens, shift, scale, wq, wk, wv, gq, gk, wo):
    seq = lax.axis_index("seq")
    head = lax.axis_index("head")
    core = seq % 2
    x_hi, y = head // 4, head % 4

    kv, normed = project_kv(tokens, shift, scale, wk, wv, gk)
    below = lax.ppermute(kv, "seq", Z_UP)
    above = lax.ppermute(kv, "seq", Z_DOWN)

    def column(side, r):
        return (((x_hi + side) % 2) * 4 + (y + r) % 4) * (OUT_COLS // 128)

    cols = jnp.stack([column(core, r) for r in range(4)] + [column(1 - core, 0)])
    q, *blocks = project_q(cols, normed, wq, gq, wo)
    q_core = lax.ppermute(q, "seq", SWAP_CORE)
    q_x = lax.ppermute(q, "seq", SWAP_X)
    first = [blocks[0]] + [lax.ppermute(blocks[r], "head", Y_STEP[r]) for r in (1, 2, 3)]
    q_xc = lax.ppermute(q_x, "seq", SWAP_CORE)
    far_a = lax.ppermute(below[:256], "seq", Z_UP)
    far_b = lax.ppermute(above[256:], "seq", Z_DOWN)
    qs = (q, q_core, q_x, q_xc)
    parts = attend_first(qs[:3], (kv, below, above))
    part, *first[1:] = lax.optimization_barrier((parts[0], *first[1:]))
    parts = [part, parts[1]]
    second = [blocks[4]] + [lax.ppermute(first[r], "seq", SWAP_CORE) for r in (1, 2, 3)]

    out = None
    for half in range(2):
        keep, send = attend_last(half, qs, (kv, below, above, far_a, far_b), parts[half])
        mine, away = combine_core(keep, lax.ppermute(send, "seq", SWAP_CORE))
        if half == 0:
            away, parts[1], *second[1:] = lax.optimization_barrier((away, parts[1], *second[1:]))
        recv = lax.ppermute(away, "seq", SWAP_X)
        att = combine_x(mine, recv)
        attended = [att] + [lax.ppermute(att, "head", Y_STEP[r]) for r in (1, 2, 3)]
        kept, sent = out_project(core, attended, first, second)
        out = finish(half, kept, lax.ppermute(sent, "head", SWAP_XHI), out)
    return out


def solution(mesh):
    in_specs = (
        P("seq", None),
        P(),
        P(),
        P(None, "head"),
        P(None, "head"),
        P(None, "head"),
        P("head"),
        P("head"),
        P("head", None),
    )
    out_specs = P("seq", "head")
    return jax.shard_map(shards, mesh=mesh, in_specs=in_specs, out_specs=out_specs, check_vma=False)
```

```python
import functools
import math

import jax
import jax.numpy as jnp
from jax import lax
from jax.experimental import pallas as pl
from jax.experimental.pallas import tpu as pltpu
from jax.sharding import PartitionSpec as P

HD = 128
SOFTCAP = 10.0
EPSILON = 1e-06
GROUP_HEADS = 3
WIDE = GROUP_HEADS * HD
ROWS = 512
D = 5120
OUT_COLS = 640
TOK_PARTS = 2
HALF = ROWS // 2
PACK = HALF + HALF // 8
EXP_SCALE = SOFTCAP * math.log2(math.e)
SCORE_SCALE = 1.0 / (SOFTCAP * math.sqrt(HD))

BF16 = jnp.bfloat16
F32 = jnp.float32


def seq_perm(move):
    pairs = []
    for i in range(16):
        x, z, c = move(i // 8, (i // 2) % 4, i % 2)
        pairs.append((i, x * 8 + (z % 4) * 2 + c))
    return pairs


def head_perm(move):
    pairs = []
    for i in range(8):
        x, y = move(i // 4, i % 4)
        pairs.append((i, x * 4 + (y % 4)))
    return pairs


SWAP_CORE = seq_perm(lambda x, z, c: (x, z, 1 - c))
SWAP_X = seq_perm(lambda x, z, c: (1 - x, z, c))
Z_UP = seq_perm(lambda x, z, c: (x, z + 1, c))
Z_DOWN = seq_perm(lambda x, z, c: (x, z - 1, c))
SWAP_XHI = head_perm(lambda x, y: (1 - x, y))
Y_STEP = [None] + [head_perm(lambda x, y, r=r: (x, y + r)) for r in (1, 2, 3)]


def params(mib=8):
    return pltpu.CompilerParams(vmem_limit_bytes=mib * 2**20)


def cost(flops, nbytes, trans=0):
    return pl.CostEstimate(flops=int(flops), bytes_accessed=int(nbytes), transcendentals=int(trans))


def unit(a):
    return a * lax.rsqrt(jnp.mean(a * a, axis=1, keepdims=True) + EPSILON)


def qkv_kernel(tok, shift_h, scale_h, wq, wk, wv, gq_h, gk_h, q_o, kv_o, tok_v, n_s, wq_v, wk_v, wv_v, shift, scale, gq, gk, tsem, wsem, vsem):
    tiles = D // 128
    part = ROWS // TOK_PARTS

    def rows_of(i):
        return pl.ds(i * part, part)

    tok_in = [pltpu.make_async_copy(tok.at[rows_of(i)], tok_v.at[rows_of(i)], tsem.at[i]) for i in range(TOK_PARTS)]
    w_in = [pltpu.make_async_copy(w, dst, wsem.at[i]) for i, (w, dst) in enumerate(((wk, wk_v), (wv, wv_v), (wq, wq_v)))]
    vec_in = [
        pltpu.make_async_copy(src, dst, vsem.at[i])
        for i, (src, dst) in enumerate(((shift_h, shift), (scale_h, scale), (gq_h, gq), (gk_h, gk)))
    ]
    for c in vec_in + tok_in:
        c.start()
    for c in vec_in:
        c.wait()

    for p in range(TOK_PARTS):
        tok_in[p].wait()
        if p == 0:
            for c in w_in:
                c.start()

        def stats(i, carry, p=p):
            rows = pl.ds(pl.multiple_of(p * part + i * 32, 32), 32)
            base = tok_v[rows, :128].astype(F32)
            s1 = jnp.zeros((32, 128), F32)
            s2 = jnp.zeros((32, 128), F32)
            for t in range(1, tiles):
                d = tok_v[rows, t * 128 : (t + 1) * 128].astype(F32) - base
                s1 = s1 + d
                s2 = s2 + d * d
            low = s1 * (1.0 / tiles)
            lane_mean = base + low
            mean = jnp.sum(lane_mean, axis=1, keepdims=True) * (1.0 / 128)
            off = lane_mean - mean
            var = jnp.sum(s2 - s1 * low + tiles * (off * off), axis=1, keepdims=True) * (1.0 / D)
            m = jnp.broadcast_to(mean, (32, 128))
            r = jnp.broadcast_to(lax.rsqrt(var + EPSILON), (32, 128))
            for t in range(tiles):
                cols = slice(t * 128, (t + 1) * 128)
                y = (tok_v[rows, cols].astype(F32) - m) * r
                n_s[rows, cols] = (y * (1.0 + scale[:, cols]) + shift[:, cols]).astype(BF16)
            return carry

        lax.fori_loop(0, part // 32, stats, 0, unroll=2)
    for c in w_in[:2]:
        c.wait()
    for h in range(GROUP_HEADS):
        cols = slice(h * HD, (h + 1) * HD)
        w = jnp.concatenate([wk_v[:, cols], wv_v[:, cols]], axis=1)
        d = jnp.dot(n_s[...], w, preferred_element_type=F32)
        at = 2 * h * HD
        kv_o[:, at : at + HD] = (unit(d[:, :HD]) * gk[cols].reshape(1, HD)).astype(BF16)
        kv_o[:, at + HD : at + 2 * HD] = d[:, HD:].astype(BF16)
    w_in[2].wait()
    d = jnp.dot(n_s[...], wq_v[...], preferred_element_type=F32)
    for h in range(GROUP_HEADS):
        cols = slice(h * HD, (h + 1) * HD)
        q_o[:, cols] = (unit(d[:, cols]) * (gq[cols] * SCORE_SCALE).reshape(1, HD)).astype(BF16)


def project(tokens, shift, scale, wq, wk, wv, gq, gk):
    hbm = pl.BlockSpec(memory_space=pltpu.HBM)
    vmem = pl.BlockSpec(memory_space=pltpu.VMEM)
    return pl.pallas_call(
        qkv_kernel,
        in_specs=[hbm] * 8,
        out_specs=[vmem, vmem],
        out_shape=[jax.ShapeDtypeStruct((ROWS, WIDE), BF16), jax.ShapeDtypeStruct((ROWS, 2 * WIDE), BF16)],
        scratch_shapes=[
            pltpu.VMEM((ROWS, D), BF16),
            pltpu.VMEM((ROWS, D), BF16),
            pltpu.VMEM((D, WIDE), BF16),
            pltpu.VMEM((D, WIDE), BF16),
            pltpu.VMEM((D, WIDE), BF16),
            pltpu.VMEM((1, D), F32),
            pltpu.VMEM((1, D), F32),
            pltpu.VMEM((WIDE,), F32),
            pltpu.VMEM((WIDE,), F32),
            pltpu.SemaphoreType.DMA((TOK_PARTS,)),
            pltpu.SemaphoreType.DMA((3,)),
            pltpu.SemaphoreType.DMA((4,)),
        ],
        compiler_params=params(60),
        cost_estimate=cost(2 * ROWS * D * WIDE * 3, 18e6),
        name="project",
    )(tokens, shift.reshape(1, D), scale.reshape(1, D), wq, wk, wv, gq, gk)


def blocks_kernel(cols, wo, own, up, down, other, sem):
    mid = WIDE // 2

    def block(i, rows, dst, j):
        src = wo.at[rows, pl.ds(pl.multiple_of(cols[i] * 128, 128), OUT_COLS)]
        return pltpu.make_async_copy(src, dst, sem.at[j])

    every = pl.ds(0, WIDE)
    copies = [
        block(1, every, up.at[every], 0),
        block(2, pl.ds(0, mid), up.at[pl.ds(WIDE, mid)], 1),
        block(3, every, down.at[every], 2),
        block(2, pl.ds(mid, mid), down.at[pl.ds(WIDE, mid)], 3),
        block(0, every, own, 4),
        block(4, every, other, 5),
    ]
    for c in copies:
        c.start()
    for c in copies:
        c.wait()


def take_blocks(cols, wo):
    return pl.pallas_call(
        blocks_kernel,
        in_specs=[pl.BlockSpec(memory_space=pltpu.SMEM), pl.BlockSpec(memory_space=pltpu.HBM)],
        out_specs=[pl.BlockSpec(memory_space=pltpu.VMEM)] * 4,
        out_shape=[jax.ShapeDtypeStruct((rows, OUT_COLS), BF16) for rows in (WIDE, WIDE * 3 // 2, WIDE * 3 // 2, WIDE)],
        scratch_shapes=[pltpu.SemaphoreType.DMA((6,))],
        compiler_params=params(60),
        cost_estimate=cost(1e6, 6e6),
        name="take_blocks",
    )(cols, wo)


def mix(qq, kvs, chunk):
    acc = None
    for kv in kvs:
        for s in range(0, kv.shape[0], chunk):
            k = kv[s : s + chunk, :HD]
            v = kv[s : s + chunk, HD:]
            x = lax.dot_general(qq, k, (((1,), (1,)), ((), ())), preferred_element_type=F32)
            p = jnp.exp2(EXP_SCALE * jnp.tanh(x)).astype(BF16)
            d = jnp.dot(p, jnp.concatenate([v, jnp.ones_like(v)], axis=1), preferred_element_type=F32)
            acc = d if acc is None else acc + d
    return acc


def first_kernel(q0, q1, q2, k0, k1, k2, part0, part1):
    for i, q in enumerate((q0, q1, q2)):
        acc = mix(q[...], (k0, k1, k2), 256)
        for half, part in enumerate((part0, part1)):
            rows = acc[half * HALF : (half + 1) * HALF]
            at = i * PACK
            part[at : at + HALF, :] = rows[:, :HD].astype(BF16)
            for p in range(HALF // 128):
                t = jnp.transpose(rows[p * 128 : (p + 1) * 128, HD:])
                to = at + HALF + 16 * p
                part[to : to + 16, :] = t[:16].astype(BF16)


def attend_first(qs, kvs):
    head = lambda rows, cols: pl.BlockSpec((rows, cols), lambda h: (0, h))
    return pl.pallas_call(
        first_kernel,
        grid=(GROUP_HEADS,),
        in_specs=[head(ROWS, HD)] * 3 + [head(ROWS, 2 * HD)] * 3,
        out_specs=[head(3 * PACK, HD)] * 2,
        out_shape=[jax.ShapeDtypeStruct((3 * PACK, WIDE), BF16)] * 2,
        compiler_params=params(24),
        cost_estimate=cost(3 * 4 * 1536 * 1536 * 256, 6e6, 3 * 2 * 1536 * 1536),
        name="attend_first",
    )(*qs, *kvs)


def last_kernel(q0, q1, q2, q3, n0, n1, n2, k0, k1, part, keep, send):
    for h in range(GROUP_HEADS):
        col = slice(h * HD, (h + 1) * HD)
        wide = slice(2 * h * HD, 2 * (h + 1) * HD)
        for i, (q, out, base) in enumerate(((q0, keep, 0), (q1, send, 0), (q2, keep, PACK), (q3, send, PACK))):
            far = (k0[:, wide], k1[:, wide])
            if i == 3:
                acc = mix(q[:, col], (n0[:, wide], n1[:, wide], n2[:, wide]) + far, 256)
                mixture, totals = acc[:, :HD], None
            else:
                acc = mix(q[:, col], far, 256)
                old = part[i * PACK : (i + 1) * PACK, col].astype(F32)
                mixture, totals = acc[:, :HD] + old[:HALF], old[HALF:]
            out[base : base + HALF, col] = mixture.astype(BF16)
            for p in range(HALF // 128):
                t = jnp.transpose(acc[p * 128 : (p + 1) * 128, HD:])[:16]
                if totals is not None:
                    t = t + totals[16 * p : 16 * (p + 1)]
                at = base + HALF + 16 * p
                out[at : at + 16, col] = t.astype(BF16)


def attend_last(half, qs, kvs, part):
    whole = lambda shape: pl.BlockSpec(shape, lambda j: (0, 0))
    return pl.pallas_call(
        last_kernel,
        grid=(1,),
        in_specs=[pl.BlockSpec((HALF, WIDE), lambda j: (half, 0))] * 4
        + [whole((ROWS, 2 * WIDE))] * 3
        + [whole((256, 2 * WIDE))] * 2
        + [whole((3 * PACK, WIDE))],
        out_specs=[whole((2 * PACK, WIDE))] * 2,
        out_shape=[jax.ShapeDtypeStruct((2 * PACK, WIDE), BF16)] * 2,
        compiler_params=params(24),
        cost_estimate=cost(3 * 4 * 1024 * 1024 * 256, 4e6, 3 * 2 * 1024 * 1024),
        name="attend_last",
    )(*qs, *kvs, part)


def combine_core_kernel(keep, recv, mine, away):
    total = keep[...].astype(F32) + recv[...].astype(F32)
    mine[...] = total[:PACK].astype(BF16)
    away[...] = total[PACK:].astype(BF16)


def combine_core(keep, recv):
    return pl.pallas_call(
        combine_core_kernel,
        out_shape=[jax.ShapeDtypeStruct((PACK, WIDE), BF16)] * 2,
        compiler_params=params(),
        cost_estimate=cost(1e6, 2e6),
        name="combine_core",
    )(keep, recv)


def combine_x_kernel(mine, recv, out):
    total = mine[...].astype(F32) + recv[...].astype(F32)
    for h in range(GROUP_HEADS):
        cols = slice(h * HD, (h + 1) * HD)
        for p in range(HALF // 128):
            rows = slice(p * 128, (p + 1) * 128)
            t = total[HALF + 16 * p : HALF + 16 * p + 1, cols]
            out[rows, cols] = (total[rows, cols] / jnp.transpose(jnp.broadcast_to(t, (128, 128)))).astype(BF16)


def combine_x(mine, recv):
    return pl.pallas_call(
        combine_x_kernel,
        out_shape=jax.ShapeDtypeStruct((HALF, WIDE), BF16),
        compiler_params=params(),
        cost_estimate=cost(1e6, 1e6),
        name="combine_x",
    )(mine, recv)


def out_kernel(core, a0, a1, a2, a3, *refs):
    first = refs[:5]
    second = refs[5:10]
    keep, send = refs[10:]
    rows = jnp.concatenate([a0[...], a1[...], a2[...], a3[...]], axis=1)
    lead = core[0] == 0

    def stacked(refs, col):
        own, up, far_up, far_down, down = refs
        pieces = [own[:, col], up[:WIDE, col], far_up[:, col], far_down[:, col], down[:WIDE, col]]
        return jnp.concatenate(pieces, axis=0)

    for t in range(OUT_COLS // 128):
        col = slice(t * 128, (t + 1) * 128)
        w = jnp.concatenate([stacked(first, col), stacked(second, col)], axis=1)
        acc = jnp.dot(rows, w, preferred_element_type=F32)
        keep[:, col] = jnp.where(lead, acc[:, :128], acc[:, 128:]).astype(BF16)
        send[:, col] = jnp.where(lead, acc[:, 128:], acc[:, :128]).astype(BF16)


def out_project(core, attended, first, second):
    vmem = pl.BlockSpec(memory_space=pltpu.VMEM)
    return pl.pallas_call(
        out_kernel,
        in_specs=[pl.BlockSpec(memory_space=pltpu.SMEM)] + [vmem] * 14,
        out_specs=[vmem, vmem],
        out_shape=[jax.ShapeDtypeStruct((HALF, OUT_COLS), BF16)] * 2,
        compiler_params=params(16),
        cost_estimate=cost(2 * HALF * 1536 * 1280, 6e6),
        name="out_project",
    )(core.reshape(1), *attended, *first, *second)


def final_kernel(keep, recv, *rest):
    rest[-1][...] = (keep[...].astype(F32) + recv[...].astype(F32)).astype(BF16)


def finish(half, keep, recv, out=None):
    whole = pl.BlockSpec((HALF, OUT_COLS), lambda j: (0, 0))
    return pl.pallas_call(
        final_kernel,
        grid=(1,),
        in_specs=[whole] * 2 + ([] if out is None else [pl.BlockSpec(memory_space=pl.ANY)]),
        out_specs=pl.BlockSpec((HALF, OUT_COLS), lambda j: (half, 0)),
        out_shape=jax.ShapeDtypeStruct((ROWS, OUT_COLS), BF16),
        input_output_aliases={} if out is None else {2: 0},
        compiler_params=params(8),
        cost_estimate=cost(1e6, 1e6),
        name="finish",
    )(*([keep, recv] if out is None else [keep, recv, out]))


def shards(tokens, shift, scale, wq, wk, wv, gq, gk, wo):
    seq = lax.axis_index("seq")
    head = lax.axis_index("head")
    core = seq % 2
    x_hi, y = head // 4, head % 4

    q, kv = project(tokens, shift, scale, wq, wk, wv, gq, gk)
    below = lax.ppermute(kv, "seq", Z_UP)
    above = lax.ppermute(kv, "seq", Z_DOWN)

    def column(side, r):
        return (((x_hi + side) % 2) * 4 + (y + r) % 4) * (OUT_COLS // 128)

    cols = jnp.stack([column(core, r) for r in range(4)] + [column(1 - core, 0)])
    q_core = lax.ppermute(q, "seq", SWAP_CORE)
    q_x = lax.ppermute(q, "seq", SWAP_X)
    q_core, cols = lax.optimization_barrier((q_core, cols))
    own, up, down, other = take_blocks(cols, wo)
    up = lax.ppermute(up, "head", Y_STEP[1])
    down = lax.ppermute(down, "head", Y_STEP[3])
    q_xc = lax.ppermute(q_x, "seq", SWAP_CORE)
    far_a = lax.ppermute(below[:256], "seq", Z_UP)
    far_b = lax.ppermute(above[256:], "seq", Z_DOWN)
    qs = (q, q_core, q_x, q_xc)
    parts = attend_first(qs[:3], (kv, below, above))
    part, up, down = lax.optimization_barrier((parts[0], up, down))
    parts = [part, parts[1]]
    second = [lax.ppermute(w, "seq", SWAP_CORE) for w in (up, down)]
    far = [lax.ppermute(up[WIDE:], "head", Y_STEP[1]), lax.ppermute(down[WIDE:], "head", Y_STEP[3])]

    out = None
    for half in range(2):
        keep, send = attend_last(half, qs, (kv, below, above, far_a, far_b), parts[half])
        mine, away = combine_core(keep, lax.ppermute(send, "seq", SWAP_CORE))
        if half == 0:
            away, parts[1] = lax.optimization_barrier((away, parts[1]))
        recv = lax.ppermute(away, "seq", SWAP_X)
        if half == 0:
            recv, *far = lax.optimization_barrier((recv, *far))
            far_core = [lax.ppermute(w, "seq", SWAP_CORE) for w in far]
        att = combine_x(mine, recv)
        attended = [att] + [lax.ppermute(att, "head", Y_STEP[r]) for r in (1, 2, 3)]
        first_w = (own, up, *far, down)
        second_w = (other, second[0], *far_core, second[1])
        kept, sent = out_project(core, attended, first_w, second_w)
        out = finish(half, kept, lax.ppermute(sent, "head", SWAP_XHI), out)
    return out


def solution(mesh):
    in_specs = (
        P("seq", None),
        P(),
        P(),
        P(None, "head"),
        P(None, "head"),
        P(None, "head"),
        P("head"),
        P("head"),
        P("head", None),
    )
    out_specs = P("seq", "head")
    return jax.shard_map(shards, mesh=mesh, in_specs=in_specs, out_specs=out_specs, check_vma=False)
```

```python
import functools
import math

import jax
import jax.numpy as jnp
from jax import lax
from jax.experimental import pallas as pl
from jax.experimental.pallas import tpu as pltpu
from jax.sharding import PartitionSpec as P

HD = 128
SOFTCAP = 10.0
EPSILON = 1e-06
GROUP_HEADS = 3
WIDE = GROUP_HEADS * HD
ROWS = 512
D = 5120
OUT_COLS = 640
TOK_PARTS = 2
HALF = ROWS // 2
PACK = HALF + HALF // 8
EXP_SCALE = SOFTCAP * math.log2(math.e)
SCORE_SCALE = 1.0 / (SOFTCAP * math.sqrt(HD))

BF16 = jnp.bfloat16
F32 = jnp.float32


def seq_perm(move):
    pairs = []
    for i in range(16):
        x, z, c = move(i // 8, (i // 2) % 4, i % 2)
        pairs.append((i, x * 8 + (z % 4) * 2 + c))
    return pairs


def head_perm(move):
    pairs = []
    for i in range(8):
        x, y = move(i // 4, i % 4)
        pairs.append((i, x * 4 + (y % 4)))
    return pairs


SWAP_CORE = seq_perm(lambda x, z, c: (x, z, 1 - c))
SWAP_X = seq_perm(lambda x, z, c: (1 - x, z, c))
Z_UP = seq_perm(lambda x, z, c: (x, z + 1, c))
Z_DOWN = seq_perm(lambda x, z, c: (x, z - 1, c))
SWAP_XHI = head_perm(lambda x, y: (1 - x, y))
Y_STEP = [None] + [head_perm(lambda x, y, r=r: (x, y + r)) for r in (1, 2, 3)]


def params(mib=8):
    return pltpu.CompilerParams(vmem_limit_bytes=mib * 2**20)


def cost(flops, nbytes, trans=0):
    return pl.CostEstimate(flops=int(flops), bytes_accessed=int(nbytes), transcendentals=int(trans))


def unit(a):
    return a * lax.rsqrt(jnp.mean(a * a, axis=1, keepdims=True) + EPSILON)


def qkv_kernel(tok, shift_h, scale_h, wq, wk, wv, gq_h, gk_h, q_o, kv_o, tok_v, n_s, wq_v, wk_v, wv_v, shift, scale, gq, gk, tsem, wsem, vsem):
    tiles = D // 128
    part = ROWS // TOK_PARTS

    def rows_of(i):
        return pl.ds(i * part, part)

    tok_in = [pltpu.make_async_copy(tok.at[rows_of(i)], tok_v.at[rows_of(i)], tsem.at[i]) for i in range(TOK_PARTS)]
    w_in = [pltpu.make_async_copy(w, dst, wsem.at[i]) for i, (w, dst) in enumerate(((wk, wk_v), (wv, wv_v), (wq, wq_v)))]
    vec_in = [
        pltpu.make_async_copy(src, dst, vsem.at[i])
        for i, (src, dst) in enumerate(((shift_h, shift), (scale_h, scale), (gq_h, gq), (gk_h, gk)))
    ]
    for c in vec_in + tok_in:
        c.start()
    for c in vec_in:
        c.wait()

    for p in range(TOK_PARTS):
        tok_in[p].wait()
        if p == 0:
            for c in w_in:
                c.start()

        def stats(i, carry, p=p):
            rows = pl.ds(pl.multiple_of(p * part + i * 32, 32), 32)
            base = tok_v[rows, :128].astype(F32)
            s1 = jnp.zeros((32, 128), F32)
            s2 = jnp.zeros((32, 128), F32)
            for t in range(1, tiles):
                d = tok_v[rows, t * 128 : (t + 1) * 128].astype(F32) - base
                s1 = s1 + d
                s2 = s2 + d * d
            low = s1 * (1.0 / tiles)
            lane_mean = base + low
            mean = jnp.sum(lane_mean, axis=1, keepdims=True) * (1.0 / 128)
            off = lane_mean - mean
            var = jnp.sum(s2 - s1 * low + tiles * (off * off), axis=1, keepdims=True) * (1.0 / D)
            m = jnp.broadcast_to(mean, (32, 128))
            r = jnp.broadcast_to(lax.rsqrt(var + EPSILON), (32, 128))
            for t in range(tiles):
                cols = slice(t * 128, (t + 1) * 128)
                y = (tok_v[rows, cols].astype(F32) - m) * r
                n_s[rows, cols] = (y * (1.0 + scale[:, cols]) + shift[:, cols]).astype(BF16)
            return carry

        lax.fori_loop(0, part // 32, stats, 0, unroll=2)
    for c in w_in[:2]:
        c.wait()
    for h in range(GROUP_HEADS):
        cols = slice(h * HD, (h + 1) * HD)
        w = jnp.concatenate([wk_v[:, cols], wv_v[:, cols]], axis=1)
        d = jnp.dot(n_s[...], w, preferred_element_type=F32)
        at = 2 * h * HD
        kv_o[:, at : at + HD] = (unit(d[:, :HD]) * gk[cols].reshape(1, HD)).astype(BF16)
        kv_o[:, at + HD : at + 2 * HD] = d[:, HD:].astype(BF16)
    w_in[2].wait()
    d = jnp.dot(n_s[...], wq_v[...], preferred_element_type=F32)
    for h in range(GROUP_HEADS):
        cols = slice(h * HD, (h + 1) * HD)
        q_o[:, cols] = (unit(d[:, cols]) * (gq[cols] * SCORE_SCALE).reshape(1, HD)).astype(BF16)


def project(tokens, shift, scale, wq, wk, wv, gq, gk):
    hbm = pl.BlockSpec(memory_space=pltpu.HBM)
    vmem = pl.BlockSpec(memory_space=pltpu.VMEM)
    return pl.pallas_call(
        qkv_kernel,
        in_specs=[hbm] * 8,
        out_specs=[vmem, vmem],
        out_shape=[jax.ShapeDtypeStruct((ROWS, WIDE), BF16), jax.ShapeDtypeStruct((ROWS, 2 * WIDE), BF16)],
        scratch_shapes=[
            pltpu.VMEM((ROWS, D), BF16),
            pltpu.VMEM((ROWS, D), BF16),
            pltpu.VMEM((D, WIDE), BF16),
            pltpu.VMEM((D, WIDE), BF16),
            pltpu.VMEM((D, WIDE), BF16),
            pltpu.VMEM((1, D), F32),
            pltpu.VMEM((1, D), F32),
            pltpu.VMEM((WIDE,), F32),
            pltpu.VMEM((WIDE,), F32),
            pltpu.SemaphoreType.DMA((TOK_PARTS,)),
            pltpu.SemaphoreType.DMA((3,)),
            pltpu.SemaphoreType.DMA((4,)),
        ],
        compiler_params=params(60),
        cost_estimate=cost(2 * ROWS * D * WIDE * 3, 18e6),
        name="project",
    )(tokens, shift.reshape(1, D), scale.reshape(1, D), wq, wk, wv, gq, gk)


def blocks_kernel(cols, wo, own, up, down, other, sem):
    mid = WIDE // 2

    def block(i, rows, dst, j):
        src = wo.at[rows, pl.ds(pl.multiple_of(cols[i] * 128, 128), OUT_COLS)]
        return pltpu.make_async_copy(src, dst, sem.at[j])

    every = pl.ds(0, WIDE)
    copies = [
        block(1, every, up.at[every], 0),
        block(2, pl.ds(0, mid), up.at[pl.ds(WIDE, mid)], 1),
        block(3, every, down.at[every], 2),
        block(2, pl.ds(mid, mid), down.at[pl.ds(WIDE, mid)], 3),
        block(0, every, own, 4),
        block(4, every, other, 5),
    ]
    for c in copies:
        c.start()
    for c in copies:
        c.wait()


def take_blocks(cols, wo):
    return pl.pallas_call(
        blocks_kernel,
        in_specs=[pl.BlockSpec(memory_space=pltpu.SMEM), pl.BlockSpec(memory_space=pltpu.HBM)],
        out_specs=[pl.BlockSpec(memory_space=pltpu.VMEM)] * 4,
        out_shape=[jax.ShapeDtypeStruct((rows, OUT_COLS), BF16) for rows in (WIDE, WIDE * 3 // 2, WIDE * 3 // 2, WIDE)],
        scratch_shapes=[pltpu.SemaphoreType.DMA((6,))],
        compiler_params=params(60),
        cost_estimate=cost(1e6, 6e6),
        name="take_blocks",
    )(cols, wo)


def mix(qq, kvs, chunk):
    acc = None
    for kv in kvs:
        for s in range(0, kv.shape[0], chunk):
            k = kv[s : s + chunk, :HD]
            v = kv[s : s + chunk, HD:]
            x = lax.dot_general(qq, k, (((1,), (1,)), ((), ())), preferred_element_type=F32)
            p = jnp.exp2(EXP_SCALE * jnp.tanh(x)).astype(BF16)
            d = jnp.dot(p, jnp.concatenate([v, jnp.ones_like(v)], axis=1), preferred_element_type=F32)
            acc = d if acc is None else acc + d
    return acc


def first_kernel(q0, q1, q2, k0, k1, k2, part0, part1):
    for i, q in enumerate((q0, q1, q2)):
        acc = mix(q[...], (k0, k1, k2), 256)
        for half, part in enumerate((part0, part1)):
            rows = acc[half * HALF : (half + 1) * HALF]
            at = i * PACK
            part[at : at + HALF, :] = rows[:, :HD].astype(BF16)
            for p in range(HALF // 128):
                t = jnp.transpose(rows[p * 128 : (p + 1) * 128, HD:])
                to = at + HALF + 16 * p
                part[to : to + 16, :] = t[:16].astype(BF16)


def attend_first(qs, kvs):
    head = lambda rows, cols: pl.BlockSpec((rows, cols), lambda h: (0, h))
    return pl.pallas_call(
        first_kernel,
        grid=(GROUP_HEADS,),
        in_specs=[head(ROWS, HD)] * 3 + [head(ROWS, 2 * HD)] * 3,
        out_specs=[head(3 * PACK, HD)] * 2,
        out_shape=[jax.ShapeDtypeStruct((3 * PACK, WIDE), BF16)] * 2,
        compiler_params=params(24),
        cost_estimate=cost(3 * 4 * 1536 * 1536 * 256, 6e6, 3 * 2 * 1536 * 1536),
        name="attend_first",
    )(*qs, *kvs)


def last_kernel(q0, q1, q2, q3, n0, n1, n2, k0, k1, part0, part1, keep, send):
    for h in range(GROUP_HEADS):
        col = slice(h * HD, (h + 1) * HD)
        wide = slice(2 * h * HD, 2 * (h + 1) * HD)
        for i, (q, out) in enumerate(((q0, keep), (q1, send), (q2, keep), (q3, send))):
            kvs = (k0[:, wide], k1[:, wide])
            if i == 3:
                kvs = (n0[:, wide], n1[:, wide], n2[:, wide]) + kvs
            acc = mix(q[:, col], kvs, 256)
            for half, part in enumerate((part0, part1)):
                rows = acc[half * HALF : (half + 1) * HALF]
                base = (2 * half + i // 2) * PACK
                mixture, old = rows[:, :HD], None
                if i < 3:
                    old = part[i * PACK : (i + 1) * PACK, col].astype(F32)
                    mixture = mixture + old[:HALF]
                out[base : base + HALF, col] = mixture.astype(BF16)
                for p in range(HALF // 128):
                    t = jnp.transpose(rows[p * 128 : (p + 1) * 128, HD:])[:16]
                    at = HALF + 16 * p
                    if i < 3:
                        t = t + old[at : at + 16]
                    out[base + at : base + at + 16, col] = t.astype(BF16)


def attend_last(qs, kvs, parts):
    whole = lambda shape: pl.BlockSpec(shape, lambda j: (0, 0))
    return pl.pallas_call(
        last_kernel,
        grid=(1,),
        in_specs=[whole(a.shape) for a in (*qs, *kvs, *parts)],
        out_specs=[whole((4 * PACK, WIDE))] * 2,
        out_shape=[jax.ShapeDtypeStruct((4 * PACK, WIDE), BF16)] * 2,
        compiler_params=params(32),
        cost_estimate=cost(3 * 4 * 2048 * 1024 * 256, 8e6, 3 * 2 * 2048 * 1024),
        name="attend_last",
    )(*qs, *kvs, *parts)


def combine_core_kernel(keep, recv, *outs):
    total = keep[...].astype(F32) + recv[...].astype(F32)
    for i, out in enumerate(outs):
        out[...] = total[i * PACK : (i + 1) * PACK].astype(BF16)


def combine_core(keep, recv):
    return pl.pallas_call(
        combine_core_kernel,
        out_shape=[jax.ShapeDtypeStruct((PACK, WIDE), BF16)] * 4,
        compiler_params=params(12),
        cost_estimate=cost(1e6, 2e6),
        name="combine_core",
    )(keep, recv)


def combine_x_kernel(mine, recv, out):
    total = mine[...].astype(F32) + recv[...].astype(F32)
    for h in range(GROUP_HEADS):
        cols = slice(h * HD, (h + 1) * HD)
        for p in range(HALF // 128):
            rows = slice(p * 128, (p + 1) * 128)
            t = total[HALF + 16 * p : HALF + 16 * p + 1, cols]
            out[rows, cols] = (total[rows, cols] / jnp.transpose(jnp.broadcast_to(t, (128, 128)))).astype(BF16)


def combine_x(mine, recv):
    return pl.pallas_call(
        combine_x_kernel,
        out_shape=jax.ShapeDtypeStruct((HALF, WIDE), BF16),
        compiler_params=params(),
        cost_estimate=cost(1e6, 1e6),
        name="combine_x",
    )(mine, recv)


def out_kernel(core, a0, a1, a2, a3, *refs):
    first = refs[:5]
    second = refs[5:10]
    keep, send = refs[10:]
    rows = jnp.concatenate([a0[...], a1[...], a2[...], a3[...]], axis=1)
    lead = core[0] == 0

    def stacked(refs, col):
        own, up, far_up, far_down, down = refs
        pieces = [own[:, col], up[:WIDE, col], far_up[:, col], far_down[:, col], down[:WIDE, col]]
        return jnp.concatenate(pieces, axis=0)

    for t in range(OUT_COLS // 128):
        col = slice(t * 128, (t + 1) * 128)
        w = jnp.concatenate([stacked(first, col), stacked(second, col)], axis=1)
        acc = jnp.dot(rows, w, preferred_element_type=F32)
        keep[:, col] = jnp.where(lead, acc[:, :128], acc[:, 128:]).astype(BF16)
        send[:, col] = jnp.where(lead, acc[:, 128:], acc[:, :128]).astype(BF16)


def out_project(core, attended, first, second):
    vmem = pl.BlockSpec(memory_space=pltpu.VMEM)
    return pl.pallas_call(
        out_kernel,
        in_specs=[pl.BlockSpec(memory_space=pltpu.SMEM)] + [vmem] * 14,
        out_specs=[vmem, vmem],
        out_shape=[jax.ShapeDtypeStruct((HALF, OUT_COLS), BF16)] * 2,
        compiler_params=params(16),
        cost_estimate=cost(2 * HALF * 1536 * 1280, 6e6),
        name="out_project",
    )(core.reshape(1), *attended, *first, *second)


def final_kernel(keep, recv, *rest):
    rest[-1][...] = (keep[...].astype(F32) + recv[...].astype(F32)).astype(BF16)


def finish(half, keep, recv, out=None):
    whole = pl.BlockSpec((HALF, OUT_COLS), lambda j: (0, 0))
    return pl.pallas_call(
        final_kernel,
        grid=(1,),
        in_specs=[whole] * 2 + ([] if out is None else [pl.BlockSpec(memory_space=pl.ANY)]),
        out_specs=pl.BlockSpec((HALF, OUT_COLS), lambda j: (half, 0)),
        out_shape=jax.ShapeDtypeStruct((ROWS, OUT_COLS), BF16),
        input_output_aliases={} if out is None else {2: 0},
        compiler_params=params(8),
        cost_estimate=cost(1e6, 1e6),
        name="finish",
    )(*([keep, recv] if out is None else [keep, recv, out]))


def shards(tokens, shift, scale, wq, wk, wv, gq, gk, wo):
    seq = lax.axis_index("seq")
    head = lax.axis_index("head")
    core = seq % 2
    x_hi, y = head // 4, head % 4

    q, kv = project(tokens, shift, scale, wq, wk, wv, gq, gk)
    below = lax.ppermute(kv, "seq", Z_UP)
    above = lax.ppermute(kv, "seq", Z_DOWN)

    def column(side, r):
        return (((x_hi + side) % 2) * 4 + (y + r) % 4) * (OUT_COLS // 128)

    cols = jnp.stack([column(core, r) for r in range(4)] + [column(1 - core, 0)])
    q_core = lax.ppermute(q, "seq", SWAP_CORE)
    q_x = lax.ppermute(q, "seq", SWAP_X)
    q_core, cols = lax.optimization_barrier((q_core, cols))
    own, up, down, other = take_blocks(cols, wo)
    up = lax.ppermute(up, "head", Y_STEP[1])
    down = lax.ppermute(down, "head", Y_STEP[3])
    q_xc = lax.ppermute(q_x, "seq", SWAP_CORE)
    far_a = lax.ppermute(below[:256], "seq", Z_UP)
    far_b = lax.ppermute(above[256:], "seq", Z_DOWN)
    qs = (q, q_core, q_x, q_xc)
    parts = attend_first(qs[:3], (kv, below, above))
    part, up, down = lax.optimization_barrier((parts[0], up, down))
    parts = [part, parts[1]]
    second = [lax.ppermute(w, "seq", SWAP_CORE) for w in (up, down)]
    far = [lax.ppermute(up[WIDE:], "head", Y_STEP[1]), lax.ppermute(down[WIDE:], "head", Y_STEP[3])]

    keep, send = attend_last(qs, (kv, below, above, far_a, far_b), parts)
    recv, *second = lax.optimization_barrier((lax.ppermute(send, "seq", SWAP_CORE), *second))
    mine0, away0, mine1, away1 = combine_core(keep, recv)
    recv0 = lax.ppermute(away0, "seq", SWAP_X)
    recv1 = lax.ppermute(away1, "seq", SWAP_X)
    recv1, *far = lax.optimization_barrier((recv1, *far))
    far_core = [lax.ppermute(w, "seq", SWAP_CORE) for w in far]
    first_w = (own, up, *far, down)
    second_w = (other, second[0], *far_core, second[1])
    out = None
    for half, (mine, recv) in enumerate(((mine0, recv0), (mine1, recv1))):
        att = combine_x(mine, recv)
        attended = [att] + [lax.ppermute(att, "head", Y_STEP[r]) for r in (1, 2, 3)]
        kept, sent = out_project(core, attended, first_w, second_w)
        out = finish(half, kept, lax.ppermute(sent, "head", SWAP_XHI), out)
    return out


def solution(mesh):
    in_specs = (
        P("seq", None),
        P(),
        P(),
        P(None, "head"),
        P(None, "head"),
        P(None, "head"),
        P("head"),
        P("head"),
        P("head", None),
    )
    out_specs = P("seq", "head")
    return jax.shard_map(shards, mesh=mesh, in_specs=in_specs, out_specs=out_specs, check_vma=False)
```

```python
import functools
import math

import jax
import jax.numpy as jnp
from jax import lax
from jax.experimental import pallas as pl
from jax.experimental.pallas import tpu as pltpu
from jax.sharding import PartitionSpec as P

HD = 128
SOFTCAP = 10.0
EPSILON = 1e-06
GROUP_HEADS = 3
WIDE = GROUP_HEADS * HD
ROWS = 512
D = 5120
OUT_COLS = 640
TOK_PARTS = 2
HALF = ROWS // 2
PACK = HALF + HALF // 8
EXP_SCALE = SOFTCAP * math.log2(math.e)
SCORE_SCALE = 1.0 / (SOFTCAP * math.sqrt(HD))

BF16 = jnp.bfloat16
F32 = jnp.float32


def seq_perm(move):
    pairs = []
    for i in range(16):
        x, z, c = move(i // 8, (i // 2) % 4, i % 2)
        pairs.append((i, x * 8 + (z % 4) * 2 + c))
    return pairs


def head_perm(move):
    pairs = []
    for i in range(8):
        x, y = move(i // 4, i % 4)
        pairs.append((i, x * 4 + (y % 4)))
    return pairs


SWAP_CORE = seq_perm(lambda x, z, c: (x, z, 1 - c))
SWAP_X = seq_perm(lambda x, z, c: (1 - x, z, c))
Z_UP = seq_perm(lambda x, z, c: (x, z + 1, c))
Z_DOWN = seq_perm(lambda x, z, c: (x, z - 1, c))
SWAP_XHI = head_perm(lambda x, y: (1 - x, y))
Y_STEP = [None] + [head_perm(lambda x, y, r=r: (x, y + r)) for r in (1, 2, 3)]


def params(mib=8):
    return pltpu.CompilerParams(vmem_limit_bytes=mib * 2**20)


def cost(flops, nbytes, trans=0):
    return pl.CostEstimate(flops=int(flops), bytes_accessed=int(nbytes), transcendentals=int(trans))


def unit(a):
    return a * lax.rsqrt(jnp.mean(a * a, axis=1, keepdims=True) + EPSILON)


def qkv_kernel(tok, shift_h, scale_h, wq, wk, wv, gq_h, gk_h, q_o, kv_o, tok_v, n_s, wq_v, wk_v, wv_v, shift, scale, gq, gk, tsem, wsem, vsem):
    tiles = D // 128
    part = ROWS // TOK_PARTS

    def rows_of(i):
        return pl.ds(i * part, part)

    tok_in = [pltpu.make_async_copy(tok.at[rows_of(i)], tok_v.at[rows_of(i)], tsem.at[i]) for i in range(TOK_PARTS)]
    w_in = [pltpu.make_async_copy(w, dst, wsem.at[i]) for i, (w, dst) in enumerate(((wk, wk_v), (wv, wv_v), (wq, wq_v)))]
    vec_in = [
        pltpu.make_async_copy(src, dst, vsem.at[i])
        for i, (src, dst) in enumerate(((shift_h, shift), (scale_h, scale), (gq_h, gq), (gk_h, gk)))
    ]
    for c in vec_in + tok_in:
        c.start()
    for c in vec_in:
        c.wait()

    for p in range(TOK_PARTS):
        tok_in[p].wait()
        if p == 0:
            for c in w_in:
                c.start()

        def stats(i, carry, p=p):
            rows = pl.ds(pl.multiple_of(p * part + i * 32, 32), 32)
            base = tok_v[rows, :128].astype(F32)
            s1 = jnp.zeros((32, 128), F32)
            s2 = jnp.zeros((32, 128), F32)
            for t in range(1, tiles):
                d = tok_v[rows, t * 128 : (t + 1) * 128].astype(F32) - base
                s1 = s1 + d
                s2 = s2 + d * d
            low = s1 * (1.0 / tiles)
            lane_mean = base + low
            mean = jnp.sum(lane_mean, axis=1, keepdims=True) * (1.0 / 128)
            off = lane_mean - mean
            var = jnp.sum(s2 - s1 * low + tiles * (off * off), axis=1, keepdims=True) * (1.0 / D)
            m = jnp.broadcast_to(mean, (32, 128))
            r = jnp.broadcast_to(lax.rsqrt(var + EPSILON), (32, 128))
            for t in range(tiles):
                cols = slice(t * 128, (t + 1) * 128)
                y = (tok_v[rows, cols].astype(F32) - m) * r
                n_s[rows, cols] = (y * (1.0 + scale[:, cols]) + shift[:, cols]).astype(BF16)
            return carry

        lax.fori_loop(0, part // 32, stats, 0, unroll=2)
    for c in w_in[:2]:
        c.wait()
    for h in range(GROUP_HEADS):
        cols = slice(h * HD, (h + 1) * HD)
        w = jnp.concatenate([wk_v[:, cols], wv_v[:, cols]], axis=1)
        d = jnp.dot(n_s[...], w, preferred_element_type=F32)
        at = 2 * h * HD
        kv_o[:, at : at + HD] = (unit(d[:, :HD]) * gk[cols].reshape(1, HD)).astype(BF16)
        kv_o[:, at + HD : at + 2 * HD] = d[:, HD:].astype(BF16)
    w_in[2].wait()
    d = jnp.dot(n_s[...], wq_v[...], preferred_element_type=F32)
    for h in range(GROUP_HEADS):
        cols = slice(h * HD, (h + 1) * HD)
        q_o[:, cols] = (unit(d[:, cols]) * (gq[cols] * SCORE_SCALE).reshape(1, HD)).astype(BF16)


def project(tokens, shift, scale, wq, wk, wv, gq, gk):
    hbm = pl.BlockSpec(memory_space=pltpu.HBM)
    vmem = pl.BlockSpec(memory_space=pltpu.VMEM)
    return pl.pallas_call(
        qkv_kernel,
        in_specs=[hbm] * 8,
        out_specs=[vmem, vmem],
        out_shape=[jax.ShapeDtypeStruct((ROWS, WIDE), BF16), jax.ShapeDtypeStruct((ROWS, 2 * WIDE), BF16)],
        scratch_shapes=[
            pltpu.VMEM((ROWS, D), BF16),
            pltpu.VMEM((ROWS, D), BF16),
            pltpu.VMEM((D, WIDE), BF16),
            pltpu.VMEM((D, WIDE), BF16),
            pltpu.VMEM((D, WIDE), BF16),
            pltpu.VMEM((1, D), F32),
            pltpu.VMEM((1, D), F32),
            pltpu.VMEM((WIDE,), F32),
            pltpu.VMEM((WIDE,), F32),
            pltpu.SemaphoreType.DMA((TOK_PARTS,)),
            pltpu.SemaphoreType.DMA((3,)),
            pltpu.SemaphoreType.DMA((4,)),
        ],
        compiler_params=params(60),
        cost_estimate=cost(2 * ROWS * D * WIDE * 3, 18e6),
        name="project",
    )(tokens, shift.reshape(1, D), scale.reshape(1, D), wq, wk, wv, gq, gk)


def blocks_kernel(cols, wo, own, up, down, other, sem):
    mid = WIDE // 2

    def block(i, rows, dst, j):
        src = wo.at[rows, pl.ds(pl.multiple_of(cols[i] * 128, 128), OUT_COLS)]
        return pltpu.make_async_copy(src, dst, sem.at[j])

    every = pl.ds(0, WIDE)
    copies = [
        block(1, every, up.at[every], 0),
        block(2, pl.ds(0, mid), up.at[pl.ds(WIDE, mid)], 1),
        block(3, every, down.at[every], 2),
        block(2, pl.ds(mid, mid), down.at[pl.ds(WIDE, mid)], 3),
        block(0, every, own, 4),
        block(4, every, other, 5),
    ]
    for c in copies:
        c.start()
    for c in copies:
        c.wait()


def take_blocks(cols, wo):
    return pl.pallas_call(
        blocks_kernel,
        in_specs=[pl.BlockSpec(memory_space=pltpu.SMEM), pl.BlockSpec(memory_space=pltpu.HBM)],
        out_specs=[pl.BlockSpec(memory_space=pltpu.VMEM)] * 4,
        out_shape=[jax.ShapeDtypeStruct((rows, OUT_COLS), BF16) for rows in (WIDE, WIDE * 3 // 2, WIDE * 3 // 2, WIDE)],
        scratch_shapes=[pltpu.SemaphoreType.DMA((6,))],
        compiler_params=params(60),
        cost_estimate=cost(1e6, 6e6),
        name="take_blocks",
    )(cols, wo)


def mix(qq, kvs, chunk):
    acc = None
    for kv in kvs:
        for s in range(0, kv.shape[0], chunk):
            k = kv[s : s + chunk, :HD]
            v = kv[s : s + chunk, HD:]
            x = lax.dot_general(qq, k, (((1,), (1,)), ((), ())), preferred_element_type=F32)
            p = jnp.exp2(EXP_SCALE * jnp.tanh(x)).astype(BF16)
            d = jnp.dot(p, jnp.concatenate([v, jnp.ones_like(v)], axis=1), preferred_element_type=F32)
            acc = d if acc is None else acc + d
    return acc


def part_kernel(n_q, n_kv, *refs):
    qs, kvs = refs[:n_q], refs[n_q : n_q + n_kv]
    parts = refs[n_q + n_kv :]
    for i, q in enumerate(qs):
        acc = mix(q[...], kvs, 256)
        for half, part in enumerate(parts):
            rows = acc[half * HALF : (half + 1) * HALF]
            at = i * PACK
            part[at : at + HALF, :] = rows[:, :HD].astype(BF16)
            for p in range(HALF // 128):
                t = jnp.transpose(rows[p * 128 : (p + 1) * 128, HD:])
                to = at + HALF + 16 * p
                part[to : to + 16, :] = t[:16].astype(BF16)


def attend_part(qs, kvs):
    head = lambda rows, cols: pl.BlockSpec((rows, cols), lambda h: (0, h))
    pairs = len(qs) * len(kvs)
    return pl.pallas_call(
        functools.partial(part_kernel, len(qs), len(kvs)),
        grid=(GROUP_HEADS,),
        in_specs=[head(ROWS, HD)] * len(qs) + [head(ROWS, 2 * HD)] * len(kvs),
        out_specs=[head(len(qs) * PACK, HD)] * 2,
        out_shape=[jax.ShapeDtypeStruct((len(qs) * PACK, WIDE), BF16)] * 2,
        compiler_params=params(24),
        cost_estimate=cost(pairs * 3 * ROWS * ROWS * 256, 1e6, 0),
        name="attend_part",
    )(*qs, *kvs)


def last_kernel(q0, q1, q2, q3, k0, k1, own0, own1, near0, near1, cross0, cross1, keep, send):
    for h in range(GROUP_HEADS):
        col = slice(h * HD, (h + 1) * HD)
        wide = slice(2 * h * HD, 2 * (h + 1) * HD)
        for i, (q, out) in enumerate(((q0, keep), (q1, send), (q2, keep), (q3, send))):
            acc = mix(q[:, col], (k0[:, wide], k1[:, wide]), 256)
            for half, (own, near, cross) in enumerate(((own0, near0, cross0), (own1, near1, cross1))):
                rows = acc[half * HALF : (half + 1) * HALF]
                base = (2 * half + i // 2) * PACK
                quarter = slice(i * PACK, (i + 1) * PACK)
                if i < 3:
                    old = own[quarter, col].astype(F32) + near[quarter, col].astype(F32)
                else:
                    old = cross[:, col].astype(F32)
                out[base : base + HALF, col] = (rows[:, :HD] + old[:HALF]).astype(BF16)
                for p in range(HALF // 128):
                    t = jnp.transpose(rows[p * 128 : (p + 1) * 128, HD:])[:16]
                    at = HALF + 16 * p
                    out[base + at : base + at + 16, col] = (t + old[at : at + 16]).astype(BF16)


def attend_last(qs, kvs, parts):
    whole = lambda shape: pl.BlockSpec(shape, lambda j: (0, 0))
    return pl.pallas_call(
        last_kernel,
        grid=(1,),
        in_specs=[whole(a.shape) for a in (*qs, *kvs, *parts)],
        out_specs=[whole((4 * PACK, WIDE))] * 2,
        out_shape=[jax.ShapeDtypeStruct((4 * PACK, WIDE), BF16)] * 2,
        compiler_params=params(32),
        cost_estimate=cost(3 * 4 * 2048 * 512 * 256, 8e6, 0),
        name="attend_last",
    )(*qs, *kvs, *parts)


def combine_core_kernel(keep, recv, *outs):
    total = keep[...].astype(F32) + recv[...].astype(F32)
    for i, out in enumerate(outs):
        out[...] = total[i * PACK : (i + 1) * PACK].astype(BF16)


def combine_core(keep, recv):
    return pl.pallas_call(
        combine_core_kernel,
        out_shape=[jax.ShapeDtypeStruct((PACK, WIDE), BF16)] * 4,
        compiler_params=params(12),
        cost_estimate=cost(1e6, 2e6),
        name="combine_core",
    )(keep, recv)


def combine_x_kernel(mine, recv, out):
    total = mine[...].astype(F32) + recv[...].astype(F32)
    for h in range(GROUP_HEADS):
        cols = slice(h * HD, (h + 1) * HD)
        for p in range(HALF // 128):
            rows = slice(p * 128, (p + 1) * 128)
            t = total[HALF + 16 * p : HALF + 16 * p + 1, cols]
            out[rows, cols] = (total[rows, cols] / jnp.transpose(jnp.broadcast_to(t, (128, 128)))).astype(BF16)


def combine_x(mine, recv):
    return pl.pallas_call(
        combine_x_kernel,
        out_shape=jax.ShapeDtypeStruct((HALF, WIDE), BF16),
        compiler_params=params(),
        cost_estimate=cost(1e6, 1e6),
        name="combine_x",
    )(mine, recv)


def out_kernel(core, a0, a1, a2, a3, *refs):
    first = refs[:5]
    second = refs[5:10]
    keep, send = refs[10:]
    rows = jnp.concatenate([a0[...], a1[...], a2[...], a3[...]], axis=1)
    lead = core[0] == 0

    def stacked(refs, col):
        own, up, far_up, far_down, down = refs
        pieces = [own[:, col], up[:WIDE, col], far_up[:, col], far_down[:, col], down[:WIDE, col]]
        return jnp.concatenate(pieces, axis=0)

    for t in range(OUT_COLS // 128):
        col = slice(t * 128, (t + 1) * 128)
        w = jnp.concatenate([stacked(first, col), stacked(second, col)], axis=1)
        acc = jnp.dot(rows, w, preferred_element_type=F32)
        keep[:, col] = jnp.where(lead, acc[:, :128], acc[:, 128:]).astype(BF16)
        send[:, col] = jnp.where(lead, acc[:, 128:], acc[:, :128]).astype(BF16)


def out_project(core, attended, first, second):
    vmem = pl.BlockSpec(memory_space=pltpu.VMEM)
    return pl.pallas_call(
        out_kernel,
        in_specs=[pl.BlockSpec(memory_space=pltpu.SMEM)] + [vmem] * 14,
        out_specs=[vmem, vmem],
        out_shape=[jax.ShapeDtypeStruct((HALF, OUT_COLS), BF16)] * 2,
        compiler_params=params(16),
        cost_estimate=cost(2 * HALF * 1536 * 1280, 6e6),
        name="out_project",
    )(core.reshape(1), *attended, *first, *second)


def final_kernel(keep, recv, *rest):
    rest[-1][...] = (keep[...].astype(F32) + recv[...].astype(F32)).astype(BF16)


def finish(half, keep, recv, out=None):
    whole = pl.BlockSpec((HALF, OUT_COLS), lambda j: (0, 0))
    return pl.pallas_call(
        final_kernel,
        grid=(1,),
        in_specs=[whole] * 2 + ([] if out is None else [pl.BlockSpec(memory_space=pl.ANY)]),
        out_specs=pl.BlockSpec((HALF, OUT_COLS), lambda j: (half, 0)),
        out_shape=jax.ShapeDtypeStruct((ROWS, OUT_COLS), BF16),
        input_output_aliases={} if out is None else {2: 0},
        compiler_params=params(8),
        cost_estimate=cost(1e6, 1e6),
        name="finish",
    )(*([keep, recv] if out is None else [keep, recv, out]))


def shards(tokens, shift, scale, wq, wk, wv, gq, gk, wo):
    seq = lax.axis_index("seq")
    head = lax.axis_index("head")
    core = seq % 2
    x_hi, y = head // 4, head % 4

    q, kv = project(tokens, shift, scale, wq, wk, wv, gq, gk)
    below = lax.ppermute(kv, "seq", Z_UP)
    above = lax.ppermute(kv, "seq", Z_DOWN)

    def column(side, r):
        return (((x_hi + side) % 2) * 4 + (y + r) % 4) * (OUT_COLS // 128)

    cols = jnp.stack([column(core, r) for r in range(4)] + [column(1 - core, 0)])
    q_core = lax.ppermute(q, "seq", SWAP_CORE)
    q_x = lax.ppermute(q, "seq", SWAP_X)
    q_core, cols = lax.optimization_barrier((q_core, cols))
    own, up, down, other = take_blocks(cols, wo)
    up = lax.ppermute(up, "head", Y_STEP[1])
    down = lax.ppermute(down, "head", Y_STEP[3])
    q_xc = lax.ppermute(q_x, "seq", SWAP_CORE)
    parts_own = attend_part((q, q_core, q_x), (kv,))
    below, above, *parts_own = lax.optimization_barrier((below, above, *parts_own))
    far_a = lax.ppermute(below[:256], "seq", Z_UP)
    far_b = lax.ppermute(above[256:], "seq", Z_DOWN)
    qs = (q, q_core, q_x, q_xc)
    parts_near = attend_part(qs[:3], (below, above))
    parts_cross = attend_part(qs[3:], (kv, below, above))
    part, up, down = lax.optimization_barrier((parts_near[0], up, down))
    parts = (*parts_own, part, parts_near[1], *parts_cross)
    second = [lax.ppermute(w, "seq", SWAP_CORE) for w in (up, down)]
    far = [lax.ppermute(up[WIDE:], "head", Y_STEP[1]), lax.ppermute(down[WIDE:], "head", Y_STEP[3])]

    keep, send = attend_last(qs, (far_a, far_b), parts)
    recv, *second = lax.optimization_barrier((lax.ppermute(send, "seq", SWAP_CORE), *second))
    mine0, away0, mine1, away1 = combine_core(keep, recv)
    recv0 = lax.ppermute(away0, "seq", SWAP_X)
    recv1 = lax.ppermute(away1, "seq", SWAP_X)
    recv1, *far = lax.optimization_barrier((recv1, *far))
    far_core = [lax.ppermute(w, "seq", SWAP_CORE) for w in far]
    first_w = (own, up, *far, down)
    second_w = (other, second[0], *far_core, second[1])
    out = None
    for half, (mine, recv) in enumerate(((mine0, recv0), (mine1, recv1))):
        att = combine_x(mine, recv)
        attended = [att] + [lax.ppermute(att, "head", Y_STEP[r]) for r in (1, 2, 3)]
        kept, sent = out_project(core, attended, first_w, second_w)
        out = finish(half, kept, lax.ppermute(sent, "head", SWAP_XHI), out)
    return out


def solution(mesh):
    in_specs = (
        P("seq", None),
        P(),
        P(),
        P(None, "head"),
        P(None, "head"),
        P(None, "head"),
        P("head"),
        P("head"),
        P("head", None),
    )
    out_specs = P("seq", "head")
    return jax.shard_map(shards, mesh=mesh, in_specs=in_specs, out_specs=out_specs, check_vma=False)
```

```python
import functools
import math

import jax
import jax.numpy as jnp
from jax import lax
from jax.experimental import pallas as pl
from jax.experimental.pallas import tpu as pltpu
from jax.sharding import PartitionSpec as P

HD = 128
SOFTCAP = 10.0
EPSILON = 1e-06
GROUP_HEADS = 3
WIDE = GROUP_HEADS * HD
ROWS = 512
D = 5120
OUT_COLS = 640
TOK_PARTS = 2
HALF = ROWS // 2
PACK = HALF + HALF // 8
EXP_SCALE = SOFTCAP * math.log2(math.e)
SCORE_SCALE = 1.0 / (SOFTCAP * math.sqrt(HD))

BF16 = jnp.bfloat16
F32 = jnp.float32


def seq_perm(move):
    pairs = []
    for i in range(16):
        x, z, c = move(i // 8, (i // 2) % 4, i % 2)
        pairs.append((i, x * 8 + (z % 4) * 2 + c))
    return pairs


def head_perm(move):
    pairs = []
    for i in range(8):
        x, y = move(i // 4, i % 4)
        pairs.append((i, x * 4 + (y % 4)))
    return pairs


SWAP_CORE = seq_perm(lambda x, z, c: (x, z, 1 - c))
SWAP_X = seq_perm(lambda x, z, c: (1 - x, z, c))
Z_UP = seq_perm(lambda x, z, c: (x, z + 1, c))
Z_DOWN = seq_perm(lambda x, z, c: (x, z - 1, c))
SWAP_XHI = head_perm(lambda x, y: (1 - x, y))
Y_STEP = [None] + [head_perm(lambda x, y, r=r: (x, y + r)) for r in (1, 2, 3)]


def params(mib=8):
    return pltpu.CompilerParams(vmem_limit_bytes=mib * 2**20)


def cost(flops, nbytes, trans=0):
    return pl.CostEstimate(flops=int(flops), bytes_accessed=int(nbytes), transcendentals=int(trans))


def unit(a):
    return a * lax.rsqrt(jnp.mean(a * a, axis=1, keepdims=True) + EPSILON)


def qkv_kernel(tok, shift_h, scale_h, wq, wk, wv, gq_h, gk_h, q_o, kv_o, tok_v, n_s, wq_v, wk_v, wv_v, shift, scale, gq, gk, tsem, wsem, vsem):
    tiles = D // 128
    part = ROWS // TOK_PARTS

    def rows_of(i):
        return pl.ds(i * part, part)

    tok_in = [pltpu.make_async_copy(tok.at[rows_of(i)], tok_v.at[rows_of(i)], tsem.at[i]) for i in range(TOK_PARTS)]
    w_in = [pltpu.make_async_copy(w, dst, wsem.at[i]) for i, (w, dst) in enumerate(((wk, wk_v), (wv, wv_v), (wq, wq_v)))]
    vec_in = [
        pltpu.make_async_copy(src, dst, vsem.at[i])
        for i, (src, dst) in enumerate(((shift_h, shift), (scale_h, scale), (gq_h, gq), (gk_h, gk)))
    ]
    for c in vec_in + tok_in:
        c.start()
    for c in vec_in:
        c.wait()

    for p in range(TOK_PARTS):
        tok_in[p].wait()
        if p == 0:
            for c in w_in:
                c.start()

        def stats(i, carry, p=p):
            rows = pl.ds(pl.multiple_of(p * part + i * 32, 32), 32)
            base = tok_v[rows, :128].astype(F32)
            s1 = jnp.zeros((32, 128), F32)
            s2 = jnp.zeros((32, 128), F32)
            for t in range(1, tiles):
                d = tok_v[rows, t * 128 : (t + 1) * 128].astype(F32) - base
                s1 = s1 + d
                s2 = s2 + d * d
            low = s1 * (1.0 / tiles)
            lane_mean = base + low
            mean = jnp.sum(lane_mean, axis=1, keepdims=True) * (1.0 / 128)
            off = lane_mean - mean
            var = jnp.sum(s2 - s1 * low + tiles * (off * off), axis=1, keepdims=True) * (1.0 / D)
            m = jnp.broadcast_to(mean, (32, 128))
            r = jnp.broadcast_to(lax.rsqrt(var + EPSILON), (32, 128))
            for t in range(tiles):
                cols = slice(t * 128, (t + 1) * 128)
                y = (tok_v[rows, cols].astype(F32) - m) * r
                n_s[rows, cols] = (y * (1.0 + scale[:, cols]) + shift[:, cols]).astype(BF16)
            return carry

        lax.fori_loop(0, part // 32, stats, 0, unroll=2)
    for c in w_in[:2]:
        c.wait()
    for h in range(GROUP_HEADS):
        cols = slice(h * HD, (h + 1) * HD)
        w = jnp.concatenate([wk_v[:, cols], wv_v[:, cols]], axis=1)
        d = jnp.dot(n_s[...], w, preferred_element_type=F32)
        at = 2 * h * HD
        kv_o[:, at : at + HD] = (unit(d[:, :HD]) * gk[cols].reshape(1, HD)).astype(BF16)
        kv_o[:, at + HD : at + 2 * HD] = d[:, HD:].astype(BF16)
    w_in[2].wait()
    d = jnp.dot(n_s[...], wq_v[...], preferred_element_type=F32)
    for h in range(GROUP_HEADS):
        cols = slice(h * HD, (h + 1) * HD)
        q_o[:, cols] = (unit(d[:, cols]) * (gq[cols] * SCORE_SCALE).reshape(1, HD)).astype(BF16)


def project(tokens, shift, scale, wq, wk, wv, gq, gk):
    hbm = pl.BlockSpec(memory_space=pltpu.HBM)
    vmem = pl.BlockSpec(memory_space=pltpu.VMEM)
    return pl.pallas_call(
        qkv_kernel,
        in_specs=[hbm] * 8,
        out_specs=[vmem, vmem],
        out_shape=[jax.ShapeDtypeStruct((ROWS, WIDE), BF16), jax.ShapeDtypeStruct((ROWS, 2 * WIDE), BF16)],
        scratch_shapes=[
            pltpu.VMEM((ROWS, D), BF16),
            pltpu.VMEM((ROWS, D), BF16),
            pltpu.VMEM((D, WIDE), BF16),
            pltpu.VMEM((D, WIDE), BF16),
            pltpu.VMEM((D, WIDE), BF16),
            pltpu.VMEM((1, D), F32),
            pltpu.VMEM((1, D), F32),
            pltpu.VMEM((WIDE,), F32),
            pltpu.VMEM((WIDE,), F32),
            pltpu.SemaphoreType.DMA((TOK_PARTS,)),
            pltpu.SemaphoreType.DMA((3,)),
            pltpu.SemaphoreType.DMA((4,)),
        ],
        compiler_params=params(60),
        cost_estimate=cost(2 * ROWS * D * WIDE * 3, 18e6),
        name="project",
    )(tokens, shift.reshape(1, D), scale.reshape(1, D), wq, wk, wv, gq, gk)


def blocks_kernel(cols, wo, own, up, down, other, sem):
    mid = WIDE // 2

    def block(i, rows, dst, j):
        src = wo.at[rows, pl.ds(pl.multiple_of(cols[i] * 128, 128), OUT_COLS)]
        return pltpu.make_async_copy(src, dst, sem.at[j])

    every = pl.ds(0, WIDE)
    copies = [
        block(1, every, up.at[every], 0),
        block(2, pl.ds(0, mid), up.at[pl.ds(WIDE, mid)], 1),
        block(3, every, down.at[every], 2),
        block(2, pl.ds(mid, mid), down.at[pl.ds(WIDE, mid)], 3),
        block(0, every, own, 4),
        block(4, every, other, 5),
    ]
    for c in copies:
        c.start()
    for c in copies:
        c.wait()


def take_blocks(cols, wo):
    return pl.pallas_call(
        blocks_kernel,
        in_specs=[pl.BlockSpec(memory_space=pltpu.SMEM), pl.BlockSpec(memory_space=pltpu.HBM)],
        out_specs=[pl.BlockSpec(memory_space=pltpu.VMEM)] * 4,
        out_shape=[jax.ShapeDtypeStruct((rows, OUT_COLS), BF16) for rows in (WIDE, WIDE * 3 // 2, WIDE * 3 // 2, WIDE)],
        scratch_shapes=[pltpu.SemaphoreType.DMA((6,))],
        compiler_params=params(60),
        cost_estimate=cost(1e6, 6e6),
        name="take_blocks",
    )(cols, wo)


def mix(qq, kvs, chunk):
    acc = None
    for kv in kvs:
        for s in range(0, kv.shape[0], chunk):
            k = kv[s : s + chunk, :HD]
            v = kv[s : s + chunk, HD:]
            x = lax.dot_general(qq, k, (((1,), (1,)), ((), ())), preferred_element_type=F32)
            p = jnp.exp2(EXP_SCALE * jnp.tanh(x)).astype(BF16)
            d = jnp.dot(p, jnp.concatenate([v, jnp.ones_like(v)], axis=1), preferred_element_type=F32)
            acc = d if acc is None else acc + d
    return acc


def part_kernel(n_q, n_kv, *refs):
    qs, kvs = refs[:n_q], refs[n_q : n_q + n_kv]
    parts = refs[n_q + n_kv :]
    for i, q in enumerate(qs):
        acc = mix(q[...], kvs, 256)
        for half, part in enumerate(parts):
            rows = acc[half * HALF : (half + 1) * HALF]
            at = i * PACK
            part[at : at + HALF, :] = rows[:, :HD].astype(BF16)
            for p in range(HALF // 128):
                t = jnp.transpose(rows[p * 128 : (p + 1) * 128, HD:])
                to = at + HALF + 16 * p
                part[to : to + 16, :] = t[:16].astype(BF16)


def attend_part(qs, kvs):
    head = lambda rows, cols: pl.BlockSpec((rows, cols), lambda h: (0, h))
    pairs = len(qs) * len(kvs)
    return pl.pallas_call(
        functools.partial(part_kernel, len(qs), len(kvs)),
        grid=(GROUP_HEADS,),
        in_specs=[head(ROWS, HD)] * len(qs) + [head(ROWS, 2 * HD)] * len(kvs),
        out_specs=[head(len(qs) * PACK, HD)] * 2,
        out_shape=[jax.ShapeDtypeStruct((len(qs) * PACK, WIDE), BF16)] * 2,
        compiler_params=params(24),
        cost_estimate=cost(pairs * 3 * ROWS * ROWS * 256, 1e6, 0),
        name="attend_part",
    )(*qs, *kvs)


def last_kernel(q0, q1, q2, q3, k0, k1, own0, own1, near0, near1, cross0, cross1, keep, send):
    for h in range(GROUP_HEADS):
        col = slice(h * HD, (h + 1) * HD)
        wide = slice(2 * h * HD, 2 * (h + 1) * HD)
        for i, (q, out) in enumerate(((q0, keep), (q1, send), (q2, keep), (q3, send))):
            acc = mix(q[:, col], (k0[:, wide], k1[:, wide]), 256)
            for half, (own, near, cross) in enumerate(((own0, near0, cross0), (own1, near1, cross1))):
                rows = acc[half * HALF : (half + 1) * HALF]
                base = (2 * half + i // 2) * PACK
                quarter = slice(i * PACK, (i + 1) * PACK)
                if i < 3:
                    old = own[quarter, col].astype(F32) + near[quarter, col].astype(F32)
                else:
                    old = cross[:, col].astype(F32)
                out[base : base + HALF, col] = (rows[:, :HD] + old[:HALF]).astype(BF16)
                for p in range(HALF // 128):
                    t = jnp.transpose(rows[p * 128 : (p + 1) * 128, HD:])[:16]
                    at = HALF + 16 * p
                    out[base + at : base + at + 16, col] = (t + old[at : at + 16]).astype(BF16)


def attend_last(qs, kvs, parts):
    whole = lambda shape: pl.BlockSpec(shape, lambda j: (0, 0))
    return pl.pallas_call(
        last_kernel,
        grid=(1,),
        in_specs=[whole(a.shape) for a in (*qs, *kvs, *parts)],
        out_specs=[whole((4 * PACK, WIDE))] * 2,
        out_shape=[jax.ShapeDtypeStruct((4 * PACK, WIDE), BF16)] * 2,
        compiler_params=params(32),
        cost_estimate=cost(3 * 4 * 2048 * 512 * 256, 8e6, 0),
        name="attend_last",
    )(*qs, *kvs, *parts)


def combine_core_kernel(keep, recv, *outs):
    total = keep[...].astype(F32) + recv[...].astype(F32)
    for i, out in enumerate(outs):
        out[...] = total[i * PACK : (i + 1) * PACK].astype(BF16)


def combine_core(keep, recv):
    return pl.pallas_call(
        combine_core_kernel,
        out_shape=[jax.ShapeDtypeStruct((PACK, WIDE), BF16)] * 4,
        compiler_params=params(12),
        cost_estimate=cost(1e6, 2e6),
        name="combine_core",
    )(keep, recv)


def combine_x_kernel(mine, recv, out):
    total = mine[...].astype(F32) + recv[...].astype(F32)
    for h in range(GROUP_HEADS):
        cols = slice(h * HD, (h + 1) * HD)
        for p in range(HALF // 128):
            rows = slice(p * 128, (p + 1) * 128)
            t = total[HALF + 16 * p : HALF + 16 * p + 1, cols]
            out[rows, cols] = (total[rows, cols] / jnp.transpose(jnp.broadcast_to(t, (128, 128)))).astype(BF16)


def combine_x(mine, recv):
    return pl.pallas_call(
        combine_x_kernel,
        out_shape=jax.ShapeDtypeStruct((HALF, WIDE), BF16),
        compiler_params=params(),
        cost_estimate=cost(1e6, 1e6),
        name="combine_x",
    )(mine, recv)


def out_kernel(core, a0, a1, a2, a3, *refs):
    first = refs[:5]
    second = refs[5:10]
    keep, send = refs[10:]
    rows = jnp.concatenate([a0[...], a1[...], a2[...], a3[...]], axis=1)
    lead = core[0] == 0

    def stacked(refs, col):
        own, up, far_up, far_down, down = refs
        pieces = [own[:, col], up[:WIDE, col], far_up[:, col], far_down[:, col], down[:WIDE, col]]
        return jnp.concatenate(pieces, axis=0)

    for t in range(OUT_COLS // 128):
        col = slice(t * 128, (t + 1) * 128)
        w = jnp.concatenate([stacked(first, col), stacked(second, col)], axis=1)
        acc = jnp.dot(rows, w, preferred_element_type=F32)
        keep[:, col] = jnp.where(lead, acc[:, :128], acc[:, 128:]).astype(BF16)
        send[:, col] = jnp.where(lead, acc[:, 128:], acc[:, :128]).astype(BF16)


def out_project(core, attended, first, second):
    vmem = pl.BlockSpec(memory_space=pltpu.VMEM)
    return pl.pallas_call(
        out_kernel,
        in_specs=[pl.BlockSpec(memory_space=pltpu.SMEM)] + [vmem] * 14,
        out_specs=[vmem, vmem],
        out_shape=[jax.ShapeDtypeStruct((HALF, OUT_COLS), BF16)] * 2,
        compiler_params=params(16),
        cost_estimate=cost(2 * HALF * 1536 * 1280, 6e6),
        name="out_project",
    )(core.reshape(1), *attended, *first, *second)


def final_kernel(keep, recv, *rest):
    rest[-1][...] = (keep[...].astype(F32) + recv[...].astype(F32)).astype(BF16)


def finish(half, keep, recv, out=None):
    whole = pl.BlockSpec((HALF, OUT_COLS), lambda j: (0, 0))
    return pl.pallas_call(
        final_kernel,
        grid=(1,),
        in_specs=[whole] * 2 + ([] if out is None else [pl.BlockSpec(memory_space=pl.ANY)]),
        out_specs=pl.BlockSpec((HALF, OUT_COLS), lambda j: (half, 0)),
        out_shape=jax.ShapeDtypeStruct((ROWS, OUT_COLS), BF16),
        input_output_aliases={} if out is None else {2: 0},
        compiler_params=params(8),
        cost_estimate=cost(1e6, 1e6),
        name="finish",
    )(*([keep, recv] if out is None else [keep, recv, out]))


def shards(tokens, shift, scale, wq, wk, wv, gq, gk, wo):
    seq = lax.axis_index("seq")
    head = lax.axis_index("head")
    core = seq % 2
    x_hi, y = head // 4, head % 4

    q, kv = project(tokens, shift, scale, wq, wk, wv, gq, gk)
    below = lax.ppermute(kv, "seq", Z_UP)
    above = lax.ppermute(kv, "seq", Z_DOWN)

    def column(side, r):
        return (((x_hi + side) % 2) * 4 + (y + r) % 4) * (OUT_COLS // 128)

    cols = jnp.stack([column(core, r) for r in range(4)] + [column(1 - core, 0)])
    q_core = lax.ppermute(q, "seq", SWAP_CORE)
    q_x = lax.ppermute(q, "seq", SWAP_X)
    q_core, cols = lax.optimization_barrier((q_core, cols))
    own, up, down, other = take_blocks(cols, wo)
    up = lax.ppermute(up, "head", Y_STEP[1])
    down = lax.ppermute(down, "head", Y_STEP[3])
    q_xc = lax.ppermute(q_x, "seq", SWAP_CORE)
    parts_own = attend_part((q, q_core, q_x), (kv,))
    below, above, *parts_own = lax.optimization_barrier((below, above, *parts_own))
    far_a = lax.ppermute(below[:256], "seq", Z_UP)
    far_b = lax.ppermute(above[256:], "seq", Z_DOWN)
    qs = (q, q_core, q_x, q_xc)
    parts_near = attend_part(qs[:3], (below, above))
    parts_cross = attend_part(qs[3:], (kv, below, above))
    part, up, down = lax.optimization_barrier((parts_near[0], up, down))
    parts = (*parts_own, part, parts_near[1], *parts_cross)
    second = [lax.ppermute(w, "seq", SWAP_CORE) for w in (up, down)]
    far = [lax.ppermute(up[WIDE:], "head", Y_STEP[1]), lax.ppermute(down[WIDE:], "head", Y_STEP[3])]

    keep, send = attend_last(qs, (far_a, far_b), parts)
    recv, *second = lax.optimization_barrier((lax.ppermute(send, "seq", SWAP_CORE), *second))
    mine0, away0, mine1, away1 = combine_core(keep, recv)
    recv0 = lax.ppermute(away0, "seq", SWAP_X)
    recv1 = lax.ppermute(away1, "seq", SWAP_X)
    far_core = [lax.ppermute(w, "seq", SWAP_CORE) for w in far]
    att0 = combine_x(mine0, recv0)
    att1 = combine_x(mine1, recv1)
    att1, *far_core = lax.optimization_barrier((att1, *far_core))
    first_w = (own, up, *far, down)
    second_w = (other, second[0], *far_core, second[1])
    out = None
    for half, att in enumerate((att0, att1)):
        attended = [att] + [lax.ppermute(att, "head", Y_STEP[r]) for r in (1, 2, 3)]
        kept, sent = out_project(core, attended, first_w, second_w)
        out = finish(half, kept, lax.ppermute(sent, "head", SWAP_XHI), out)
    return out


def solution(mesh):
    in_specs = (
        P("seq", None),
        P(),
        P(),
        P(None, "head"),
        P(None, "head"),
        P(None, "head"),
        P("head"),
        P("head"),
        P("head", None),
    )
    out_specs = P("seq", "head")
    return jax.shard_map(shards, mesh=mesh, in_specs=in_specs, out_specs=out_specs, check_vma=False)
```

```python
import functools
import math

import jax
import jax.numpy as jnp
from jax import lax
from jax.experimental import pallas as pl
from jax.experimental.pallas import tpu as pltpu
from jax.sharding import PartitionSpec as P

HD = 128
SOFTCAP = 10.0
EPSILON = 1e-06
GROUP_HEADS = 3
WIDE = GROUP_HEADS * HD
ROWS = 512
D = 5120
OUT_COLS = 640
TOK_PARTS = 2
HALF = ROWS // 2
PACK = HALF + HALF // 8
EXP_SCALE = SOFTCAP * math.log2(math.e)
SCORE_SCALE = 1.0 / (SOFTCAP * math.sqrt(HD))

BF16 = jnp.bfloat16
F32 = jnp.float32


def seq_perm(move):
    pairs = []
    for i in range(16):
        x, z, c = move(i // 8, (i // 2) % 4, i % 2)
        pairs.append((i, x * 8 + (z % 4) * 2 + c))
    return pairs


def head_perm(move):
    pairs = []
    for i in range(8):
        x, y = move(i // 4, i % 4)
        pairs.append((i, x * 4 + (y % 4)))
    return pairs


SWAP_CORE = seq_perm(lambda x, z, c: (x, z, 1 - c))
SWAP_X = seq_perm(lambda x, z, c: (1 - x, z, c))
Z_UP = seq_perm(lambda x, z, c: (x, z + 1, c))
Z_DOWN = seq_perm(lambda x, z, c: (x, z - 1, c))
SWAP_XHI = head_perm(lambda x, y: (1 - x, y))
Y_STEP = [None] + [head_perm(lambda x, y, r=r: (x, y + r)) for r in (1, 2, 3)]


def params(mib=8):
    return pltpu.CompilerParams(vmem_limit_bytes=mib * 2**20)


def cost(flops, nbytes, trans=0):
    return pl.CostEstimate(flops=int(flops), bytes_accessed=int(nbytes), transcendentals=int(trans))


def unit(a):
    return a * lax.rsqrt(jnp.mean(a * a, axis=1, keepdims=True) + EPSILON)


def qkv_kernel(tok, shift_h, scale_h, wq, wk, wv, gq_h, gk_h, q_o, kv_o, tok_v, n_s, wq_v, wk_v, wv_v, shift, scale, gq, gk, tsem, wsem, vsem):
    tiles = D // 128
    part = ROWS // TOK_PARTS

    def rows_of(i):
        return pl.ds(i * part, part)

    tok_in = [pltpu.make_async_copy(tok.at[rows_of(i)], tok_v.at[rows_of(i)], tsem.at[i]) for i in range(TOK_PARTS)]
    w_in = [pltpu.make_async_copy(w, dst, wsem.at[i]) for i, (w, dst) in enumerate(((wk, wk_v), (wv, wv_v), (wq, wq_v)))]
    vec_in = [
        pltpu.make_async_copy(src, dst, vsem.at[i])
        for i, (src, dst) in enumerate(((shift_h, shift), (scale_h, scale), (gq_h, gq), (gk_h, gk)))
    ]
    for c in vec_in + tok_in:
        c.start()
    for c in vec_in:
        c.wait()

    for p in range(TOK_PARTS):
        tok_in[p].wait()
        if p == 0:
            for c in w_in:
                c.start()

        def stats(i, carry, p=p):
            rows = pl.ds(pl.multiple_of(p * part + i * 32, 32), 32)
            base = tok_v[rows, :128].astype(F32)
            s1 = jnp.zeros((32, 128), F32)
            s2 = jnp.zeros((32, 128), F32)
            for t in range(1, tiles):
                d = tok_v[rows, t * 128 : (t + 1) * 128].astype(F32) - base
                s1 = s1 + d
                s2 = s2 + d * d
            low = s1 * (1.0 / tiles)
            lane_mean = base + low
            mean = jnp.sum(lane_mean, axis=1, keepdims=True) * (1.0 / 128)
            off = lane_mean - mean
            var = jnp.sum(s2 - s1 * low + tiles * (off * off), axis=1, keepdims=True) * (1.0 / D)
            m = jnp.broadcast_to(mean, (32, 128))
            r = jnp.broadcast_to(lax.rsqrt(var + EPSILON), (32, 128))
            for t in range(tiles):
                cols = slice(t * 128, (t + 1) * 128)
                y = (tok_v[rows, cols].astype(F32) - m) * r
                n_s[rows, cols] = (y * (1.0 + scale[:, cols]) + shift[:, cols]).astype(BF16)
            return carry

        lax.fori_loop(0, part // 32, stats, 0, unroll=2)
    for c in w_in[:2]:
        c.wait()
    for h in range(GROUP_HEADS):
        cols = slice(h * HD, (h + 1) * HD)
        w = jnp.concatenate([wk_v[:, cols], wv_v[:, cols]], axis=1)
        d = jnp.dot(n_s[...], w, preferred_element_type=F32)
        at = 2 * h * HD
        kv_o[:, at : at + HD] = (unit(d[:, :HD]) * gk[cols].reshape(1, HD)).astype(BF16)
        kv_o[:, at + HD : at + 2 * HD] = d[:, HD:].astype(BF16)
    w_in[2].wait()
    d = jnp.dot(n_s[...], wq_v[...], preferred_element_type=F32)
    for h in range(GROUP_HEADS):
        cols = slice(h * HD, (h + 1) * HD)
        q_o[:, cols] = (unit(d[:, cols]) * (gq[cols] * SCORE_SCALE).reshape(1, HD)).astype(BF16)


def project(tokens, shift, scale, wq, wk, wv, gq, gk):
    hbm = pl.BlockSpec(memory_space=pltpu.HBM)
    vmem = pl.BlockSpec(memory_space=pltpu.VMEM)
    return pl.pallas_call(
        qkv_kernel,
        in_specs=[hbm] * 8,
        out_specs=[vmem, vmem],
        out_shape=[jax.ShapeDtypeStruct((ROWS, WIDE), BF16), jax.ShapeDtypeStruct((ROWS, 2 * WIDE), BF16)],
        scratch_shapes=[
            pltpu.VMEM((ROWS, D), BF16),
            pltpu.VMEM((ROWS, D), BF16),
            pltpu.VMEM((D, WIDE), BF16),
            pltpu.VMEM((D, WIDE), BF16),
            pltpu.VMEM((D, WIDE), BF16),
            pltpu.VMEM((1, D), F32),
            pltpu.VMEM((1, D), F32),
            pltpu.VMEM((WIDE,), F32),
            pltpu.VMEM((WIDE,), F32),
            pltpu.SemaphoreType.DMA((TOK_PARTS,)),
            pltpu.SemaphoreType.DMA((3,)),
            pltpu.SemaphoreType.DMA((4,)),
        ],
        compiler_params=params(60),
        cost_estimate=cost(2 * ROWS * D * WIDE * 3, 18e6),
        name="project",
    )(tokens, shift.reshape(1, D), scale.reshape(1, D), wq, wk, wv, gq, gk)


def blocks_kernel(cols, wo, own, up, down, other, sem):
    mid = WIDE // 2

    def block(i, rows, dst, j):
        src = wo.at[rows, pl.ds(pl.multiple_of(cols[i] * 128, 128), OUT_COLS)]
        return pltpu.make_async_copy(src, dst, sem.at[j])

    every = pl.ds(0, WIDE)
    copies = [
        block(1, every, up.at[every], 0),
        block(2, pl.ds(0, mid), up.at[pl.ds(WIDE, mid)], 1),
        block(3, every, down.at[every], 2),
        block(2, pl.ds(mid, mid), down.at[pl.ds(WIDE, mid)], 3),
        block(0, every, own, 4),
        block(4, every, other, 5),
    ]
    for c in copies:
        c.start()
    for c in copies:
        c.wait()


def take_blocks(cols, wo):
    return pl.pallas_call(
        blocks_kernel,
        in_specs=[pl.BlockSpec(memory_space=pltpu.SMEM), pl.BlockSpec(memory_space=pltpu.HBM)],
        out_specs=[pl.BlockSpec(memory_space=pltpu.VMEM)] * 4,
        out_shape=[jax.ShapeDtypeStruct((rows, OUT_COLS), BF16) for rows in (WIDE, WIDE * 3 // 2, WIDE * 3 // 2, WIDE)],
        scratch_shapes=[pltpu.SemaphoreType.DMA((6,))],
        compiler_params=params(60),
        cost_estimate=cost(1e6, 6e6),
        name="take_blocks",
    )(cols, wo)


def mix(qq, kvs, chunk):
    acc = None
    for kv in kvs:
        for s in range(0, kv.shape[0], chunk):
            k = kv[s : s + chunk, :HD]
            v = kv[s : s + chunk, HD:]
            x = lax.dot_general(qq, k, (((1,), (1,)), ((), ())), preferred_element_type=F32)
            p = jnp.exp2(EXP_SCALE * jnp.tanh(x)).astype(BF16)
            d = jnp.dot(p, jnp.concatenate([v, jnp.ones_like(v)], axis=1), preferred_element_type=F32)
            acc = d if acc is None else acc + d
    return acc


def part_kernel(n_q, n_kv, *refs):
    qs, kvs = refs[:n_q], refs[n_q : n_q + n_kv]
    parts = refs[n_q + n_kv :]
    for i, q in enumerate(qs):
        acc = mix(q[...], kvs, 256)
        for half, part in enumerate(parts):
            rows = acc[half * HALF : (half + 1) * HALF]
            at = i * PACK
            part[at : at + HALF, :] = rows[:, :HD].astype(BF16)
            for p in range(HALF // 128):
                t = jnp.transpose(rows[p * 128 : (p + 1) * 128, HD:])
                to = at + HALF + 16 * p
                part[to : to + 16, :] = t[:16].astype(BF16)


def attend_part(qs, kvs):
    head = lambda rows, cols: pl.BlockSpec((rows, cols), lambda h: (0, h))
    pairs = len(qs) * len(kvs)
    return pl.pallas_call(
        functools.partial(part_kernel, len(qs), len(kvs)),
        grid=(GROUP_HEADS,),
        in_specs=[head(ROWS, HD)] * len(qs) + [head(ROWS, 2 * HD)] * len(kvs),
        out_specs=[head(len(qs) * PACK, HD)] * 2,
        out_shape=[jax.ShapeDtypeStruct((len(qs) * PACK, WIDE), BF16)] * 2,
        compiler_params=params(24),
        cost_estimate=cost(pairs * 3 * ROWS * ROWS * 256, 1e6, 0),
        name="attend_part",
    )(*qs, *kvs)


def last_kernel(q0, q1, q2, q3, k0, k1, own0, own1, near0, near1, cross0, cross1, keep, send):
    for h in range(GROUP_HEADS):
        col = slice(h * HD, (h + 1) * HD)
        wide = slice(2 * h * HD, 2 * (h + 1) * HD)
        for i, (q, out) in enumerate(((q0, keep), (q1, send), (q2, keep), (q3, send))):
            acc = mix(q[:, col], (k0[:, wide], k1[:, wide]), 256)
            for half, (own, near, cross) in enumerate(((own0, near0, cross0), (own1, near1, cross1))):
                rows = acc[half * HALF : (half + 1) * HALF]
                base = (2 * half + i // 2) * PACK
                quarter = slice((i % 2) * PACK, (i % 2 + 1) * PACK)
                if i < 2:
                    old = own[quarter, col].astype(F32) + near[quarter, col].astype(F32)
                else:
                    old = cross[quarter, col].astype(F32)
                out[base : base + HALF, col] = (rows[:, :HD] + old[:HALF]).astype(BF16)
                for p in range(HALF // 128):
                    t = jnp.transpose(rows[p * 128 : (p + 1) * 128, HD:])[:16]
                    at = HALF + 16 * p
                    out[base + at : base + at + 16, col] = (t + old[at : at + 16]).astype(BF16)


def attend_last(qs, kvs, parts):
    whole = lambda shape: pl.BlockSpec(shape, lambda j: (0, 0))
    return pl.pallas_call(
        last_kernel,
        grid=(1,),
        in_specs=[whole(a.shape) for a in (*qs, *kvs, *parts)],
        out_specs=[whole((4 * PACK, WIDE))] * 2,
        out_shape=[jax.ShapeDtypeStruct((4 * PACK, WIDE), BF16)] * 2,
        compiler_params=params(32),
        cost_estimate=cost(3 * 4 * 2048 * 512 * 256, 8e6, 0),
        name="attend_last",
    )(*qs, *kvs, *parts)


def combine_core_kernel(keep, recv, *outs):
    total = keep[...].astype(F32) + recv[...].astype(F32)
    for i, out in enumerate(outs):
        out[...] = total[i * PACK : (i + 1) * PACK].astype(BF16)


def combine_core(keep, recv):
    return pl.pallas_call(
        combine_core_kernel,
        out_shape=[jax.ShapeDtypeStruct((PACK, WIDE), BF16)] * 4,
        compiler_params=params(12),
        cost_estimate=cost(1e6, 2e6),
        name="combine_core",
    )(keep, recv)


def combine_x_kernel(mine, recv, out):
    total = mine[...].astype(F32) + recv[...].astype(F32)
    for h in range(GROUP_HEADS):
        cols = slice(h * HD, (h + 1) * HD)
        for p in range(HALF // 128):
            rows = slice(p * 128, (p + 1) * 128)
            t = total[HALF + 16 * p : HALF + 16 * p + 1, cols]
            out[rows, cols] = (total[rows, cols] / jnp.transpose(jnp.broadcast_to(t, (128, 128)))).astype(BF16)


def combine_x(mine, recv):
    return pl.pallas_call(
        combine_x_kernel,
        out_shape=jax.ShapeDtypeStruct((HALF, WIDE), BF16),
        compiler_params=params(),
        cost_estimate=cost(1e6, 1e6),
        name="combine_x",
    )(mine, recv)


def out_kernel(core, a0, a1, a2, a3, *refs):
    first = refs[:5]
    second = refs[5:10]
    keep, send = refs[10:]
    rows = jnp.concatenate([a0[...], a1[...], a2[...], a3[...]], axis=1)
    lead = core[0] == 0

    def stacked(refs, col):
        own, up, far_up, far_down, down = refs
        pieces = [own[:, col], up[:WIDE, col], far_up[:, col], far_down[:, col], down[:WIDE, col]]
        return jnp.concatenate(pieces, axis=0)

    for t in range(OUT_COLS // 128):
        col = slice(t * 128, (t + 1) * 128)
        w = jnp.concatenate([stacked(first, col), stacked(second, col)], axis=1)
        acc = jnp.dot(rows, w, preferred_element_type=F32)
        keep[:, col] = jnp.where(lead, acc[:, :128], acc[:, 128:]).astype(BF16)
        send[:, col] = jnp.where(lead, acc[:, 128:], acc[:, :128]).astype(BF16)


def out_project(core, attended, first, second):
    vmem = pl.BlockSpec(memory_space=pltpu.VMEM)
    return pl.pallas_call(
        out_kernel,
        in_specs=[pl.BlockSpec(memory_space=pltpu.SMEM)] + [vmem] * 14,
        out_specs=[vmem, vmem],
        out_shape=[jax.ShapeDtypeStruct((HALF, OUT_COLS), BF16)] * 2,
        compiler_params=params(16),
        cost_estimate=cost(2 * HALF * 1536 * 1280, 6e6),
        name="out_project",
    )(core.reshape(1), *attended, *first, *second)


def final_kernel(keep, recv, *rest):
    rest[-1][...] = (keep[...].astype(F32) + recv[...].astype(F32)).astype(BF16)


def finish(half, keep, recv, out=None):
    whole = pl.BlockSpec((HALF, OUT_COLS), lambda j: (0, 0))
    return pl.pallas_call(
        final_kernel,
        grid=(1,),
        in_specs=[whole] * 2 + ([] if out is None else [pl.BlockSpec(memory_space=pl.ANY)]),
        out_specs=pl.BlockSpec((HALF, OUT_COLS), lambda j: (half, 0)),
        out_shape=jax.ShapeDtypeStruct((ROWS, OUT_COLS), BF16),
        input_output_aliases={} if out is None else {2: 0},
        compiler_params=params(8),
        cost_estimate=cost(1e6, 1e6),
        name="finish",
    )(*([keep, recv] if out is None else [keep, recv, out]))


def shards(tokens, shift, scale, wq, wk, wv, gq, gk, wo):
    seq = lax.axis_index("seq")
    head = lax.axis_index("head")
    core = seq % 2
    x_hi, y = head // 4, head % 4

    q, kv = project(tokens, shift, scale, wq, wk, wv, gq, gk)
    below = lax.ppermute(kv, "seq", Z_UP)
    above = lax.ppermute(kv, "seq", Z_DOWN)

    def column(side, r):
        return (((x_hi + side) % 2) * 4 + (y + r) % 4) * (OUT_COLS // 128)

    cols = jnp.stack([column(core, r) for r in range(4)] + [column(1 - core, 0)])
    q_core = lax.ppermute(q, "seq", SWAP_CORE)
    q_x = lax.ppermute(q, "seq", SWAP_X)
    q_core, cols = lax.optimization_barrier((q_core, cols))
    own, up, down, other = take_blocks(cols, wo)
    up = lax.ppermute(up, "head", Y_STEP[1])
    down = lax.ppermute(down, "head", Y_STEP[3])
    q_xc = lax.ppermute(q_x, "seq", SWAP_CORE)
    parts_own = attend_part((q, q_core), (kv,))
    below, above, *parts_own = lax.optimization_barrier((below, above, *parts_own))
    far_a = lax.ppermute(below[:256], "seq", Z_UP)
    far_b = lax.ppermute(above[256:], "seq", Z_DOWN)
    qs = (q, q_core, q_x, q_xc)
    parts_near = attend_part(qs[:2], (below, above))
    parts_cross = attend_part(qs[2:], (kv, below, above))
    part, up, down = lax.optimization_barrier((parts_near[0], up, down))
    parts = (*parts_own, part, parts_near[1], *parts_cross)
    second = [lax.ppermute(w, "seq", SWAP_CORE) for w in (up, down)]
    far = [lax.ppermute(up[WIDE:], "head", Y_STEP[1]), lax.ppermute(down[WIDE:], "head", Y_STEP[3])]

    keep, send = attend_last(qs, (far_a, far_b), parts)
    recv, *second = lax.optimization_barrier((lax.ppermute(send, "seq", SWAP_CORE), *second))
    mine0, away0, mine1, away1 = combine_core(keep, recv)
    recv0 = lax.ppermute(away0, "seq", SWAP_X)
    recv1 = lax.ppermute(away1, "seq", SWAP_X)
    recv1, *far = lax.optimization_barrier((recv1, *far))
    far_core = [lax.ppermute(w, "seq", SWAP_CORE) for w in far]
    first_w = (own, up, *far, down)
    second_w = (other, second[0], *far_core, second[1])
    out = None
    for half, (mine, recv) in enumerate(((mine0, recv0), (mine1, recv1))):
        att = combine_x(mine, recv)
        attended = [att] + [lax.ppermute(att, "head", Y_STEP[r]) for r in (1, 2, 3)]
        kept, sent = out_project(core, attended, first_w, second_w)
        out = finish(half, kept, lax.ppermute(sent, "head", SWAP_XHI), out)
    return out


def solution(mesh):
    in_specs = (
        P("seq", None),
        P(),
        P(),
        P(None, "head"),
        P(None, "head"),
        P(None, "head"),
        P("head"),
        P("head"),
        P("head", None),
    )
    out_specs = P("seq", "head")
    return jax.shard_map(shards, mesh=mesh, in_specs=in_specs, out_specs=out_specs, check_vma=False)
```

```python
import functools
import math

import jax
import jax.numpy as jnp
from jax import lax
from jax.experimental import pallas as pl
from jax.experimental.pallas import tpu as pltpu
from jax.sharding import PartitionSpec as P

HD = 128
SOFTCAP = 10.0
EPSILON = 1e-06
GROUP_HEADS = 3
WIDE = GROUP_HEADS * HD
ROWS = 512
D = 5120
OUT_COLS = 640
TOK_PARTS = 2
HALF = ROWS // 2
PACK = HALF + HALF // 8
EXP_SCALE = SOFTCAP * math.log2(math.e)
SCORE_SCALE = 1.0 / (SOFTCAP * math.sqrt(HD))

BF16 = jnp.bfloat16
F32 = jnp.float32


def seq_perm(move):
    pairs = []
    for i in range(16):
        x, z, c = move(i // 8, (i // 2) % 4, i % 2)
        pairs.append((i, x * 8 + (z % 4) * 2 + c))
    return pairs


def head_perm(move):
    pairs = []
    for i in range(8):
        x, y = move(i // 4, i % 4)
        pairs.append((i, x * 4 + (y % 4)))
    return pairs


SWAP_CORE = seq_perm(lambda x, z, c: (x, z, 1 - c))
SWAP_X = seq_perm(lambda x, z, c: (1 - x, z, c))
Z_UP = seq_perm(lambda x, z, c: (x, z + 1, c))
Z_DOWN = seq_perm(lambda x, z, c: (x, z - 1, c))
SWAP_XHI = head_perm(lambda x, y: (1 - x, y))
Y_STEP = [None] + [head_perm(lambda x, y, r=r: (x, y + r)) for r in (1, 2, 3)]


def params(mib=8):
    return pltpu.CompilerParams(vmem_limit_bytes=mib * 2**20)


def cost(flops, nbytes, trans=0):
    return pl.CostEstimate(flops=int(flops), bytes_accessed=int(nbytes), transcendentals=int(trans))


def unit(a):
    return a * lax.rsqrt(jnp.mean(a * a, axis=1, keepdims=True) + EPSILON)


def qkv_kernel(tok, shift_h, scale_h, wq, wk, wv, gq_h, gk_h, q_o, kv_o, tok_v, n_s, wq_v, wk_v, wv_v, shift, scale, gq, gk, tsem, wsem, vsem):
    tiles = D // 128
    part = ROWS // TOK_PARTS

    def rows_of(i):
        return pl.ds(i * part, part)

    tok_in = [pltpu.make_async_copy(tok.at[rows_of(i)], tok_v.at[rows_of(i)], tsem.at[i]) for i in range(TOK_PARTS)]
    w_in = [pltpu.make_async_copy(w, dst, wsem.at[i]) for i, (w, dst) in enumerate(((wk, wk_v), (wv, wv_v), (wq, wq_v)))]
    vec_in = [
        pltpu.make_async_copy(src, dst, vsem.at[i])
        for i, (src, dst) in enumerate(((shift_h, shift), (scale_h, scale), (gq_h, gq), (gk_h, gk)))
    ]
    for c in vec_in + tok_in:
        c.start()
    for c in vec_in:
        c.wait()

    for p in range(TOK_PARTS):
        tok_in[p].wait()
        if p == 0:
            for c in w_in:
                c.start()

        def stats(i, carry, p=p):
            rows = pl.ds(pl.multiple_of(p * part + i * 32, 32), 32)
            base = tok_v[rows, :128].astype(F32)
            s1 = jnp.zeros((32, 128), F32)
            s2 = jnp.zeros((32, 128), F32)
            for t in range(1, tiles):
                d = tok_v[rows, t * 128 : (t + 1) * 128].astype(F32) - base
                s1 = s1 + d
                s2 = s2 + d * d
            low = s1 * (1.0 / tiles)
            lane_mean = base + low
            mean = jnp.sum(lane_mean, axis=1, keepdims=True) * (1.0 / 128)
            off = lane_mean - mean
            var = jnp.sum(s2 - s1 * low + tiles * (off * off), axis=1, keepdims=True) * (1.0 / D)
            m = jnp.broadcast_to(mean, (32, 128))
            r = jnp.broadcast_to(lax.rsqrt(var + EPSILON), (32, 128))
            for t in range(tiles):
                cols = slice(t * 128, (t + 1) * 128)
                y = (tok_v[rows, cols].astype(F32) - m) * r
                n_s[rows, cols] = (y * (1.0 + scale[:, cols]) + shift[:, cols]).astype(BF16)
            return carry

        lax.fori_loop(0, part // 32, stats, 0, unroll=2)
    for c in w_in[:2]:
        c.wait()
    for h in range(GROUP_HEADS):
        cols = slice(h * HD, (h + 1) * HD)
        w = jnp.concatenate([wk_v[:, cols], wv_v[:, cols]], axis=1)
        d = jnp.dot(n_s[...], w, preferred_element_type=F32)
        at = 2 * h * HD
        kv_o[:, at : at + HD] = (unit(d[:, :HD]) * gk[cols].reshape(1, HD)).astype(BF16)
        kv_o[:, at + HD : at + 2 * HD] = d[:, HD:].astype(BF16)
    w_in[2].wait()
    d = jnp.dot(n_s[...], wq_v[...], preferred_element_type=F32)
    for h in range(GROUP_HEADS):
        cols = slice(h * HD, (h + 1) * HD)
        q_o[:, cols] = (unit(d[:, cols]) * (gq[cols] * SCORE_SCALE).reshape(1, HD)).astype(BF16)


def project(tokens, shift, scale, wq, wk, wv, gq, gk):
    hbm = pl.BlockSpec(memory_space=pltpu.HBM)
    vmem = pl.BlockSpec(memory_space=pltpu.VMEM)
    return pl.pallas_call(
        qkv_kernel,
        in_specs=[hbm] * 8,
        out_specs=[vmem, vmem],
        out_shape=[jax.ShapeDtypeStruct((ROWS, WIDE), BF16), jax.ShapeDtypeStruct((ROWS, 2 * WIDE), BF16)],
        scratch_shapes=[
            pltpu.VMEM((ROWS, D), BF16),
            pltpu.VMEM((ROWS, D), BF16),
            pltpu.VMEM((D, WIDE), BF16),
            pltpu.VMEM((D, WIDE), BF16),
            pltpu.VMEM((D, WIDE), BF16),
            pltpu.VMEM((1, D), F32),
            pltpu.VMEM((1, D), F32),
            pltpu.VMEM((WIDE,), F32),
            pltpu.VMEM((WIDE,), F32),
            pltpu.SemaphoreType.DMA((TOK_PARTS,)),
            pltpu.SemaphoreType.DMA((3,)),
            pltpu.SemaphoreType.DMA((4,)),
        ],
        compiler_params=params(60),
        cost_estimate=cost(2 * ROWS * D * WIDE * 3, 18e6),
        name="project",
    )(tokens, shift.reshape(1, D), scale.reshape(1, D), wq, wk, wv, gq, gk)


def blocks_kernel(cols, wo, own, up, down, other, sem):
    mid = WIDE // 2

    def block(i, rows, dst, j):
        src = wo.at[rows, pl.ds(pl.multiple_of(cols[i] * 128, 128), OUT_COLS)]
        return pltpu.make_async_copy(src, dst, sem.at[j])

    every = pl.ds(0, WIDE)
    copies = [
        block(1, every, up.at[every], 0),
        block(2, pl.ds(0, mid), up.at[pl.ds(WIDE, mid)], 1),
        block(3, every, down.at[every], 2),
        block(2, pl.ds(mid, mid), down.at[pl.ds(WIDE, mid)], 3),
        block(0, every, own, 4),
        block(4, every, other, 5),
    ]
    for c in copies:
        c.start()
    for c in copies:
        c.wait()


def take_blocks(cols, wo):
    return pl.pallas_call(
        blocks_kernel,
        in_specs=[pl.BlockSpec(memory_space=pltpu.SMEM), pl.BlockSpec(memory_space=pltpu.HBM)],
        out_specs=[pl.BlockSpec(memory_space=pltpu.VMEM)] * 4,
        out_shape=[jax.ShapeDtypeStruct((rows, OUT_COLS), BF16) for rows in (WIDE, WIDE * 3 // 2, WIDE * 3 // 2, WIDE)],
        scratch_shapes=[pltpu.SemaphoreType.DMA((6,))],
        compiler_params=params(60),
        cost_estimate=cost(1e6, 6e6),
        name="take_blocks",
    )(cols, wo)


def mix(qq, kvs, chunk):
    acc = None
    for kv in kvs:
        for s in range(0, kv.shape[0], chunk):
            k = kv[s : s + chunk, :HD]
            v = kv[s : s + chunk, HD:]
            x = lax.dot_general(qq, k, (((1,), (1,)), ((), ())), preferred_element_type=F32)
            p = jnp.exp2(EXP_SCALE * jnp.tanh(x)).astype(BF16)
            d = jnp.dot(p, jnp.concatenate([v, jnp.ones_like(v)], axis=1), preferred_element_type=F32)
            acc = d if acc is None else acc + d
    return acc


def part_kernel(n_q, n_kv, *refs):
    qs, kvs = refs[:n_q], refs[n_q : n_q + n_kv]
    parts = refs[n_q + n_kv :]
    for i, q in enumerate(qs):
        acc = mix(q[...], kvs, 256)
        for half, part in enumerate(parts):
            rows = acc[half * HALF : (half + 1) * HALF]
            at = i * PACK
            part[at : at + HALF, :] = rows[:, :HD].astype(BF16)
            for p in range(HALF // 128):
                t = jnp.transpose(rows[p * 128 : (p + 1) * 128, HD:])
                to = at + HALF + 16 * p
                part[to : to + 16, :] = t[:16].astype(BF16)


def attend_part(qs, kvs):
    head = lambda rows, cols: pl.BlockSpec((rows, cols), lambda h: (0, h))
    pairs = len(qs) * len(kvs)
    return pl.pallas_call(
        functools.partial(part_kernel, len(qs), len(kvs)),
        grid=(GROUP_HEADS,),
        in_specs=[head(ROWS, HD)] * len(qs) + [head(ROWS, 2 * HD)] * len(kvs),
        out_specs=[head(len(qs) * PACK, HD)] * 2,
        out_shape=[jax.ShapeDtypeStruct((len(qs) * PACK, WIDE), BF16)] * 2,
        compiler_params=params(24),
        cost_estimate=cost(pairs * 3 * ROWS * ROWS * 256, 1e6, 0),
        name="attend_part",
    )(*qs, *kvs)


def last_kernel(q0, q1, q2, q3, k0, k1, own0, own1, near0, near1, keep, send):
    for h in range(GROUP_HEADS):
        col = slice(h * HD, (h + 1) * HD)
        wide = slice(2 * h * HD, 2 * (h + 1) * HD)
        for i, (q, out) in enumerate(((q0, keep), (q1, send), (q2, keep), (q3, send))):
            acc = mix(q[:, col], (k0[:, wide], k1[:, wide]), 256)
            for half, (own, near) in enumerate(((own0, near0), (own1, near1))):
                rows = acc[half * HALF : (half + 1) * HALF]
                base = (2 * half + i // 2) * PACK
                quarter = slice(i * PACK, (i + 1) * PACK)
                old = own[quarter, col].astype(F32) + near[quarter, col].astype(F32)
                out[base : base + HALF, col] = (rows[:, :HD] + old[:HALF]).astype(BF16)
                for p in range(HALF // 128):
                    t = jnp.transpose(rows[p * 128 : (p + 1) * 128, HD:])[:16]
                    at = HALF + 16 * p
                    out[base + at : base + at + 16, col] = (t + old[at : at + 16]).astype(BF16)


def attend_last(qs, kvs, parts):
    whole = lambda shape: pl.BlockSpec(shape, lambda j: (0, 0))
    return pl.pallas_call(
        last_kernel,
        grid=(1,),
        in_specs=[whole(a.shape) for a in (*qs, *kvs, *parts)],
        out_specs=[whole((4 * PACK, WIDE))] * 2,
        out_shape=[jax.ShapeDtypeStruct((4 * PACK, WIDE), BF16)] * 2,
        compiler_params=params(32),
        cost_estimate=cost(3 * 4 * 2048 * 512 * 256, 8e6, 0),
        name="attend_last",
    )(*qs, *kvs, *parts)


def combine_core_kernel(keep, recv, *outs):
    total = keep[...].astype(F32) + recv[...].astype(F32)
    for i, out in enumerate(outs):
        out[...] = total[i * PACK : (i + 1) * PACK].astype(BF16)


def combine_core(keep, recv):
    return pl.pallas_call(
        combine_core_kernel,
        out_shape=[jax.ShapeDtypeStruct((PACK, WIDE), BF16)] * 4,
        compiler_params=params(12),
        cost_estimate=cost(1e6, 2e6),
        name="combine_core",
    )(keep, recv)


def combine_x_kernel(mine, recv, out):
    total = mine[...].astype(F32) + recv[...].astype(F32)
    for h in range(GROUP_HEADS):
        cols = slice(h * HD, (h + 1) * HD)
        for p in range(HALF // 128):
            rows = slice(p * 128, (p + 1) * 128)
            t = total[HALF + 16 * p : HALF + 16 * p + 1, cols]
            out[rows, cols] = (total[rows, cols] / jnp.transpose(jnp.broadcast_to(t, (128, 128)))).astype(BF16)


def combine_x(mine, recv):
    return pl.pallas_call(
        combine_x_kernel,
        out_shape=jax.ShapeDtypeStruct((HALF, WIDE), BF16),
        compiler_params=params(),
        cost_estimate=cost(1e6, 1e6),
        name="combine_x",
    )(mine, recv)


def out_kernel(core, a0, a1, a2, a3, *refs):
    first = refs[:5]
    second = refs[5:10]
    keep, send = refs[10:]
    rows = jnp.concatenate([a0[...], a1[...], a2[...], a3[...]], axis=1)
    lead = core[0] == 0

    def stacked(refs, col):
        own, up, far_up, far_down, down = refs
        pieces = [own[:, col], up[:WIDE, col], far_up[:, col], far_down[:, col], down[:WIDE, col]]
        return jnp.concatenate(pieces, axis=0)

    for t in range(OUT_COLS // 128):
        col = slice(t * 128, (t + 1) * 128)
        w = jnp.concatenate([stacked(first, col), stacked(second, col)], axis=1)
        acc = jnp.dot(rows, w, preferred_element_type=F32)
        keep[:, col] = jnp.where(lead, acc[:, :128], acc[:, 128:]).astype(BF16)
        send[:, col] = jnp.where(lead, acc[:, 128:], acc[:, :128]).astype(BF16)


def out_project(core, attended, first, second):
    vmem = pl.BlockSpec(memory_space=pltpu.VMEM)
    return pl.pallas_call(
        out_kernel,
        in_specs=[pl.BlockSpec(memory_space=pltpu.SMEM)] + [vmem] * 14,
        out_specs=[vmem, vmem],
        out_shape=[jax.ShapeDtypeStruct((HALF, OUT_COLS), BF16)] * 2,
        compiler_params=params(16),
        cost_estimate=cost(2 * HALF * 1536 * 1280, 6e6),
        name="out_project",
    )(core.reshape(1), *attended, *first, *second)


def final_kernel(keep, recv, *rest):
    rest[-1][...] = (keep[...].astype(F32) + recv[...].astype(F32)).astype(BF16)


def finish(half, keep, recv, out=None):
    whole = pl.BlockSpec((HALF, OUT_COLS), lambda j: (0, 0))
    return pl.pallas_call(
        final_kernel,
        grid=(1,),
        in_specs=[whole] * 2 + ([] if out is None else [pl.BlockSpec(memory_space=pl.ANY)]),
        out_specs=pl.BlockSpec((HALF, OUT_COLS), lambda j: (half, 0)),
        out_shape=jax.ShapeDtypeStruct((ROWS, OUT_COLS), BF16),
        input_output_aliases={} if out is None else {2: 0},
        compiler_params=params(8),
        cost_estimate=cost(1e6, 1e6),
        name="finish",
    )(*([keep, recv] if out is None else [keep, recv, out]))


def shards(tokens, shift, scale, wq, wk, wv, gq, gk, wo):
    seq = lax.axis_index("seq")
    head = lax.axis_index("head")
    core = seq % 2
    x_hi, y = head // 4, head % 4

    q, kv = project(tokens, shift, scale, wq, wk, wv, gq, gk)
    below = lax.ppermute(kv, "seq", Z_UP)
    above = lax.ppermute(kv, "seq", Z_DOWN)

    def column(side, r):
        return (((x_hi + side) % 2) * 4 + (y + r) % 4) * (OUT_COLS // 128)

    cols = jnp.stack([column(core, r) for r in range(4)] + [column(1 - core, 0)])
    q_core = lax.ppermute(q, "seq", SWAP_CORE)
    q_x = lax.ppermute(q, "seq", SWAP_X)
    q_core, cols = lax.optimization_barrier((q_core, cols))
    own, up, down, other = take_blocks(cols, wo)
    up = lax.ppermute(up, "head", Y_STEP[1])
    down = lax.ppermute(down, "head", Y_STEP[3])
    q_xc = lax.ppermute(q_x, "seq", SWAP_CORE)
    parts_own = attend_part((q, q_core, q_x, q_xc), (kv,))
    below, above, *parts_own = lax.optimization_barrier((below, above, *parts_own))
    far_a = lax.ppermute(below[:256], "seq", Z_UP)
    far_b = lax.ppermute(above[256:], "seq", Z_DOWN)
    qs = (q, q_core, q_x, q_xc)
    parts_near = attend_part(qs, (below, above))
    part, up, down = lax.optimization_barrier((parts_near[0], up, down))
    parts = (*parts_own, part, parts_near[1])
    second = [lax.ppermute(w, "seq", SWAP_CORE) for w in (up, down)]
    far = [lax.ppermute(up[WIDE:], "head", Y_STEP[1]), lax.ppermute(down[WIDE:], "head", Y_STEP[3])]

    keep, send = attend_last(qs, (far_a, far_b), parts)
    recv, *second = lax.optimization_barrier((lax.ppermute(send, "seq", SWAP_CORE), *second))
    mine0, away0, mine1, away1 = combine_core(keep, recv)
    recv0 = lax.ppermute(away0, "seq", SWAP_X)
    recv1 = lax.ppermute(away1, "seq", SWAP_X)
    recv1, *far = lax.optimization_barrier((recv1, *far))
    far_core = [lax.ppermute(w, "seq", SWAP_CORE) for w in far]
    first_w = (own, up, *far, down)
    second_w = (other, second[0], *far_core, second[1])
    out = None
    for half, (mine, recv) in enumerate(((mine0, recv0), (mine1, recv1))):
        att = combine_x(mine, recv)
        attended = [att] + [lax.ppermute(att, "head", Y_STEP[r]) for r in (1, 2, 3)]
        kept, sent = out_project(core, attended, first_w, second_w)
        out = finish(half, kept, lax.ppermute(sent, "head", SWAP_XHI), out)
    return out


def solution(mesh):
    in_specs = (
        P("seq", None),
        P(),
        P(),
        P(None, "head"),
        P(None, "head"),
        P(None, "head"),
        P("head"),
        P("head"),
        P("head", None),
    )
    out_specs = P("seq", "head")
    return jax.shard_map(shards, mesh=mesh, in_specs=in_specs, out_specs=out_specs, check_vma=False)
```
